256 devices in a mesh: tm: 4 (over y), chan: 64 (over x, z, core).
Axes of the slice: x: 4, y: 4, z: 8, core: 2. Of those that a mesh axis runs over, the one named last changes fastest.
Arguments:
- records: bfloat16 [256, 2048, 256], P('tm', 'chan'), may hold values from -6 to 6
- pair_blocks: int32 [1024, 2], P('chan'), may hold values from 0 to 127, as said below
- pair_counts: int32 [64], P('chan'), may hold values from 1 to 16, as said below
Outputs:
- correlations: float32 [1024, 401, 256], P(('chan', 'tm'))
The draws below stay inside these ranges and needn't reach their ends.
Inputs may be any that keep to these rules, and one draw needn't show every extreme that they name: `pair_blocks`: for owner o, every slot has 0 <= j - i < 8, j < 128, and block i among the channels of chan index o or o + 1. `pair_counts`: some owner has all its slots live in every draw.
All inputs are finite; a program needn't handle non-finite values.
Results may differ from the reference program's by a relative error of at most 0.0027.
Values may be sent and summed in bfloat16 or wider, within the bound.
No kernel may reach another device: no remote copies, remote signals or barrier semaphores. Data moves between devices by JAX's collectives and lax.ppermute only.
A program may use at most 128 MiB of HBM per device.

```python
import math
import jax
import jax.numpy as jnp
from jax import lax

NFFT = 512
SEG = 256
LAGS = 401
BLK = 16
BAND = 128
CH_DEV = 32
PB_SLOTS = 16
SEGS = 256
CHANNELS = 2048
SLOTS = 1024
N_CHAN = 64


def draw_pair_blocks(key, part):
    key = jax.random.fold_in(key, 11)
    key_first, key_second = jax.random.split(key)
    block_total = CH_DEV * N_CHAN // BLK
    owners = jnp.arange(N_CHAN * PB_SLOTS, dtype=jnp.int32) // PB_SLOTS
    reach_span = jnp.where(owners == N_CHAN - 1, 2, 4).astype(jnp.int32)
    first_block = 2 * owners + jax.random.randint(key_first, owners.shape, 0, reach_span, dtype=jnp.int32)
    first_block = first_block.at[0].set(0)
    headroom = jnp.minimum(BAND // BLK, block_total - first_block).astype(jnp.int32)
    second_block = first_block + jax.random.randint(key_second, owners.shape, 0, headroom, dtype=jnp.int32)
    last_slot = (N_CHAN - 1) * PB_SLOTS
    second_block = second_block.at[last_slot].set(block_total - 1)
    return jnp.stack([first_block, second_block], axis=1).astype(jnp.int32)


def draw_pair_counts(key, part):
    key = jax.random.fold_in(key, 12)
    key_counts, key_fullest = jax.random.split(key)
    lowest = max(1, PB_SLOTS // 8)
    counts = jax.random.randint(key_counts, (N_CHAN,), lowest, PB_SLOTS + 1, dtype=jnp.int32)
    fullest = jax.random.randint(key_fullest, (), 0, N_CHAN, dtype=jnp.int32)
    return counts.at[fullest].set(PB_SLOTS).astype(jnp.int32)


def block_levels(key, extent, pieces, smallest, largest):
    def one(position, shards_of):
        steps = jax.random.uniform(jax.random.fold_in(jax.random.fold_in(key, 6), position), (shards_of,), jnp.float32, smallest / len(pieces), largest / len(pieces))
        return jnp.repeat(jnp.exp(steps), extent[position] // shards_of).reshape((-1,) + (1,) * (len(extent) - position - 1))

    gain = one(*pieces[0])
    for cut in pieces[1:]:
        gain = gain * one(*cut)
    return gain


def scatter_about(own_key, shape, spread, most, shards=(), kind=jnp.bfloat16):
    gain = block_levels(own_key, shape, shards, -0.22, 0.18) if shards else 1.0
    array = jax.random.normal(own_key, shape, jnp.float32) * spread * gain
    return jnp.minimum(jnp.maximum(array, -most), most).astype(kind)


def setup_inputs(seed: int = 0) -> dict:
    keys = jax.random.split(jax.random.key(seed), 4)
    records = scatter_about(keys[0], (SEGS, CHANNELS, SEG), 1.0, 6.0, ((0, 4), (1, 64)))
    pair_blocks = draw_pair_blocks(jax.random.fold_in(keys[3], 71), 0)
    pair_counts = draw_pair_counts(jax.random.fold_in(keys[3], 71), 0)
    return {"records": records, "pair_blocks": pair_blocks, "pair_counts": pair_counts}


water_share = 0.1
tiny_eps = 1e-06

def make_tables(length, lag_count, segments):
    bins = length // 2
    time_index = jnp.arange(bins, dtype=jnp.int32)[:, None]
    freq_index = jnp.arange(bins, dtype=jnp.int32)[None, :]
    radians = (time_index * freq_index % length).astype(jnp.float32) * (2.0 * math.pi / length)
    forward = jnp.concatenate([jnp.cos(radians), -jnp.sin(radians)], axis=1).astype(jnp.bfloat16)
    lag_shift = jnp.arange(lag_count, dtype=jnp.int32)[:, None] - (lag_count - 1) // 2
    lag_radians = (lag_shift * freq_index % length).astype(jnp.float32) * (2.0 * math.pi / length)
    weight = jnp.where(freq_index == 0, 1.0, 2.0).astype(jnp.float32) / math.sqrt(float(bins * segments))
    backward = jnp.concatenate([jnp.cos(lag_radians) * weight, -jnp.sin(lag_radians) * weight], axis=1)
    return (forward, backward)

def whiten(records, forward):
    spectra = jnp.einsum('sct,tf->scf', records.astype(jnp.float32), forward.astype(jnp.float32), precision=lax.Precision.HIGHEST)
    bins = spectra.shape[-1] // 2
    real_part = spectra[..., :bins]
    imag_part = spectra[..., bins:]
    energy = real_part * real_part + imag_part * imag_part
    water_level = lax.optimization_barrier(jnp.mean(energy, axis=-1, keepdims=True))
    inverse_amp = 1.0 / jnp.sqrt(energy + water_share * water_level + tiny_eps)
    return jnp.concatenate([real_part * inverse_amp, imag_part * inverse_amp], axis=-1).astype(jnp.bfloat16)

def cross_spectrum(left_block, right_block):
    bins = left_block.shape[-1] // 2
    left_real = left_block[..., :bins].astype(jnp.float32)
    left_imag = left_block[..., bins:].astype(jnp.float32)
    right_real = right_block[..., :bins].astype(jnp.float32)
    right_imag = right_block[..., bins:].astype(jnp.float32)
    hp = lax.Precision.HIGHEST
    real_sum = jnp.einsum('saf,sbf->fab', left_real, right_real, precision=hp) + jnp.einsum('saf,sbf->fab', left_imag, right_imag, precision=hp)
    imag_sum = jnp.einsum('saf,sbf->fab', left_imag, right_real, precision=hp) - jnp.einsum('saf,sbf->fab', left_real, right_imag, precision=hp)
    return jnp.concatenate([real_sum.reshape(bins, -1), imag_sum.reshape(bins, -1)], axis=0)

def reference(records, pair_blocks, pair_counts):
    forward, backward = make_tables(NFFT, LAGS, SEGS)
    whitened = lax.map(lambda single: whiten(single[None], forward)[0], records)

    def per_slot(slot_index):
        owner_index = slot_index // PB_SLOTS
        first_start = (pair_blocks[slot_index, 0] * BLK).astype(jnp.int32)
        second_start = (pair_blocks[slot_index, 1] * BLK).astype(jnp.int32)
        left_block = lax.dynamic_slice_in_dim(whitened, first_start, BLK, 1)
        right_block = lax.dynamic_slice_in_dim(whitened, second_start, BLK, 1)
        cross = cross_spectrum(left_block, right_block)
        stacked = jnp.dot(backward, cross, precision=lax.Precision.HIGHEST)
        is_live = slot_index % PB_SLOTS < pair_counts[owner_index]
        return jnp.where(is_live, stacked, jnp.zeros_like(stacked))
    return lax.map(per_slot, jnp.arange(SLOTS, dtype=jnp.int32))
```

```python
import functools
import math

import jax
import jax.numpy as jnp
import ml_dtypes
import numpy as np
from jax import lax
from jax.experimental import pallas as pl
from jax.experimental.pallas import tpu as pltpu
from jax.sharding import PartitionSpec as P

LAGS = 401
ROWS = 416
BLK = 16
SLOTS = 16
BINS = 256
LEFT = 64
BAND = 176
CHUNKS = 2

water_share = 0.1
tiny_eps = 1e-06

MIB = 1024 * 1024


def make_tables(segments):
    length = 2 * BINS
    index = np.arange(BINS, dtype=np.int32)
    scale = np.float32(2.0 * math.pi / length)
    radians = (index[:, None] * index[None, :] % length).astype(np.float32) * scale
    forward = np.concatenate([np.cos(radians), -np.sin(radians)], axis=1)
    lag_shift = np.arange(LAGS, dtype=np.int32)[:, None] - (LAGS - 1) // 2
    lag_radians = (lag_shift * index[None, :] % length).astype(np.float32) * scale
    weight = np.where(index == 0, 1.0, 2.0).astype(np.float32)[None, :] / np.float32(
        math.sqrt(float(BINS * segments))
    )
    backward = np.concatenate([np.cos(lag_radians) * weight, -np.sin(lag_radians) * weight], axis=1)
    backward = np.pad(backward.astype(np.float32), ((0, ROWS - LAGS), (0, 0)))
    high = backward.astype(ml_dtypes.bfloat16)
    low = (backward - high.astype(np.float32)).astype(ml_dtypes.bfloat16)
    stacked = np.concatenate([high, high, low], axis=1)
    return (np.ascontiguousarray(forward.astype(ml_dtypes.bfloat16).T), stacked)


def front_kernel(right_ref, odd_ref, first_ref, table_ref, x0, b0, a1, b1, a2, b2, o5, out_ref,
                 band, spec_a, spec_b, bins_ref):
    segs = x0.shape[0]
    depth = 2 * segs
    odd = odd_ref[0] == 1

    @pl.loop(0, segs)
    def _(s):
        band[s, 0:32, :] = x0[s]
        band[s, 32:64, :] = jnp.where(odd, b1[s], b0[s])
        band[s, 64:96, :] = a1[s]
        band[s, 96:128, :] = jnp.where(odd, b2[s], b1[s])
        band[s, 128:160, :] = a2[s]
        band[s, 160:176, :] = o5[s]

    starts = [pl.multiple_of(right_ref[q] * BLK, BLK) for q in range(SLOTS)]

    def transform(s, spec):
        left = band[s, 0:LEFT, :]
        rows = [band[s, pl.ds(start, BLK), :] for start in starts] + [left, left]
        spec[...] = lax.dot_general(
            table_ref[...],
            jnp.concatenate(rows, axis=0),
            (((1,), (1,)), ((), ())),
            preferred_element_type=jnp.float32,
        )

    in_first = lax.broadcasted_iota(jnp.int32, (8, 128), 1) < LEFT

    def whiten(s, spec):
        for h in range(3):
            lanes = slice(h * 128, (h + 1) * 128)
            total = jnp.zeros((8, 128), jnp.float32)
            for f in range(0, BINS, 8):
                real_part = spec[f:f + 8, lanes]
                imag_part = spec[BINS + f:BINS + f + 8, lanes]
                total = total + (real_part * real_part + imag_part * imag_part)
            level = jnp.sum(total, axis=0, keepdims=True) * (1.0 / BINS)
            floor = jnp.broadcast_to(water_share * level + tiny_eps, (8, 128))
            for f in range(0, BINS, 8):
                real_part = spec[f:f + 8, lanes]
                imag_part = spec[BINS + f:BINS + f + 8, lanes]
                inverse = lax.rsqrt(real_part * real_part + imag_part * imag_part + floor)
                real_part = real_part * inverse
                imag_part = imag_part * inverse
                if h == 2:
                    real_part, imag_part = (
                        jnp.where(in_first, real_part, imag_part),
                        jnp.where(in_first, imag_part, -real_part),
                    )
                bins_ref[h, pl.ds(f * depth + s, 8, stride=depth), :] = real_part
                bins_ref[h, pl.ds(f * depth + segs + s, 8, stride=depth), :] = imag_part

    transform(0, spec_a)

    @pl.loop(0, segs // 2)
    def _(pair):
        s = 2 * pair
        transform(s + 1, spec_b)
        whiten(s, spec_a)
        transform(jnp.minimum(s + 2, segs - 1), spec_a)
        whiten(s + 1, spec_b)

    first = first_ref[...]
    chosen = [jnp.broadcast_to(first == i, (BLK, 256)) for i in range(3)]

    @pl.loop(0, BINS // 4)
    def _(group):
        for step in range(4):
            f = group * 4 + step
            rows = pl.ds(pl.multiple_of(f * depth, 8), depth)
            right = jnp.concatenate([bins_ref[0, rows, :], bins_ref[1, rows, :]], axis=1)
            left = bins_ref[2, rows, :]
            cross = lax.dot_general(
                left.astype(jnp.bfloat16),
                right.astype(jnp.bfloat16),
                (((0,), (0,)), ((), ())),
                preferred_element_type=jnp.float32,
            )
            for part in range(2):
                blocks = [cross[part * LEFT + i * BLK:part * LEFT + (i + 1) * BLK] for i in range(4)]
                own = blocks[3]
                for i in range(3):
                    own = jnp.where(chosen[i], blocks[i], own)
                for a in range(0, BLK, 8):
                    for h in range(2):
                        out_ref[h, pl.ds(a * 512 + part * BINS + f, 8, stride=512), :] = own[
                            a:a + 8, h * 128:(h + 1) * 128
                        ]


def front(right, odd, first, table, pieces):
    segs = pieces[0].shape[0]
    vmem = pl.BlockSpec(memory_space=pltpu.VMEM)
    smem = pl.BlockSpec(memory_space=pltpu.SMEM)
    return pl.pallas_call(
        front_kernel,
        out_shape=jax.ShapeDtypeStruct((2, BLK * 512, 128), jnp.float32),
        in_specs=[smem, smem] + [vmem] * (2 + len(pieces)),
        out_specs=vmem,
        scratch_shapes=[
            pltpu.VMEM((segs, BAND, BINS), jnp.bfloat16),
            pltpu.VMEM((512, 384), jnp.float32),
            pltpu.VMEM((512, 384), jnp.float32),
            pltpu.VMEM((3, BINS * 2 * segs, 128), jnp.float32),
        ],
        compiler_params=pltpu.CompilerParams(vmem_limit_bytes=56 * MIB),
        cost_estimate=pl.CostEstimate(flops=25_000_000_000, bytes_accessed=12_000_000, transcendentals=0),
        name="front",
    )(right, odd, first, table, *pieces)


def post_kernel(live_ref, table_ref, *refs):
    sums = refs[:CHUNKS]
    plus_ref, minus_ref, keep_ref, other_ref, own_ref, lags = refs[CHUNKS:]
    a = pl.program_id(0)
    halves = []
    for h in range(2):
        half = sums[0][h]
        for other in sums[1:]:
            half = half + other[h]
        halves.append(half)
    cross = jnp.concatenate(halves, axis=1)
    high = cross.astype(jnp.bfloat16)
    low = (cross - high.astype(jnp.float32)).astype(jnp.bfloat16)
    lags[a] = jnp.dot(
        table_ref[...],
        jnp.concatenate([high, low, high], axis=0),
        preferred_element_type=jnp.float32,
    )

    @pl.when(a == BLK - 1)
    def _():
        block = lax.broadcasted_iota(jnp.int32, (BLK, 128), 1) // BLK
        odd_block = {d: (block // d) % 2 == 1 for d in (4, 2, 1)}
        live = [live_ref[q] == 1 for q in range(SLOTS)]

        @pl.loop(0, ROWS // BLK)
        def _(tile):
            rows = pl.ds(pl.multiple_of(tile * BLK, BLK), BLK)
            for hq in range(2):
                for ha in range(2):
                    arrays = [lags[8 * ha + k, rows, hq * 128:(hq + 1) * 128] for k in range(8)]
                    for d in (4, 2, 1):
                        for k in range(8):
                            if k & d == 0:
                                one, two = arrays[k], arrays[k + d]
                                mask = odd_block[d]
                                arrays[k] = jnp.where(mask, pltpu.roll(two, BLK * d, 1), one)
                                arrays[k + d] = jnp.where(mask, two, pltpu.roll(one, 128 - BLK * d, 1))
                    lanes = slice(ha * 128, (ha + 1) * 128)
                    for k in range(8):
                        q = 8 * hq + k
                        value = jnp.where(live[q], arrays[k], 0.0)
                        if q < 4:
                            plus_ref[q, rows, lanes] = value.astype(jnp.bfloat16)
                        elif q < 8:
                            minus_ref[q - 4, rows, lanes] = value.astype(jnp.bfloat16)
                        elif q < 10:
                            keep_ref[q - 8, rows, lanes] = value
                        elif q < 12:
                            other_ref[q - 10, rows, lanes] = value
                        else:
                            own_ref[q - 12, rows, lanes] = value


def post(live, table, sums):
    def whole(shape):
        return pl.BlockSpec(shape, lambda a: (0,) * len(shape))

    shapes = [((4, ROWS, 256), jnp.bfloat16)] * 2 + [((2, ROWS, 256), jnp.float32)] * 2
    shapes.append(((4, ROWS, 256), jnp.float32))
    return pl.pallas_call(
        post_kernel,
        grid=(BLK,),
        out_shape=[jax.ShapeDtypeStruct(s, d) for s, d in shapes],
        in_specs=[pl.BlockSpec(memory_space=pltpu.SMEM), whole(table.shape)]
        + [pl.BlockSpec((2, 512, 128), lambda a: (0, a, 0))] * len(sums),
        out_specs=[whole(s) for s, _ in shapes],
        scratch_shapes=[pltpu.VMEM((BLK, ROWS, 256), jnp.float32)],
        compiler_params=pltpu.CompilerParams(vmem_limit_bytes=48 * MIB),
        cost_estimate=pl.CostEstimate(flops=12_000_000_000, bytes_accessed=24_000_000, transcendentals=0),
        name="post",
    )(live, table, *sums)


def moved(block, axis, to):
    size = lax.axis_size(axis)
    return lax.ppermute(block, axis, [(i, to(i) % size) for i in range(size)])


def gather_band(own):
    one_chip = functools.partial(moved, axis="chan", to=lambda i: i - 2)
    swap = functools.partial(moved, axis="chan", to=lambda i: i ^ 1)
    b0 = swap(own)
    a1 = one_chip(own)
    a2 = one_chip(a1)
    b1 = swap(a1)
    b2 = swap(a2)
    o5 = moved(a2[:, :BLK], "chan", lambda i: i - 1)
    return [own, b0, a1, b1, a2, b2, o5]


def local(records, pair_blocks, pair_counts):
    segs = records.shape[0]
    table, backward = make_tables(segs * lax.axis_size("tm"))
    owner = lax.axis_index("chan")
    row = lax.axis_index("tm")

    group = np.array([2, 2, 1, 1, 2, 2, 3, 3, 1, 1, 3, 3, 0, 0, 0, 0], np.int32)
    inside = np.array([0, 1, 2, 3, 2, 3, 0, 1, 0, 1, 2, 3, 0, 1, 2, 3], np.int32)
    order = (row + group) % 4 * 4 + inside
    relative = pair_blocks[order] - 2 * owner
    first = jnp.clip(relative[:, 0], 0, 3)
    right = jnp.clip(relative[:, 1], 0, 10)
    live = (order < pair_counts[0]).astype(jnp.int32)
    odd = (owner % 2).astype(jnp.int32)[None]
    first_lanes = jnp.repeat(first, BLK)[None, :]

    step = segs // CHUNKS
    sums = []
    for chunk in range(CHUNKS):
        pieces = gather_band(records[chunk * step:(chunk + 1) * step])
        sums.append(front(right, odd, first_lanes, table, pieces))
    plus, minus, keep, other, own = post(live, backward, sums)

    from_below = moved(plus, "tm", lambda i: i + 1)
    from_above = moved(minus, "tm", lambda i: i - 1)
    up = (keep + from_below[:2].astype(jnp.float32)).astype(jnp.bfloat16)
    down = (other + from_above[:2].astype(jnp.float32)).astype(jnp.bfloat16)
    two_below = moved(up, "tm", lambda i: i + 1)
    two_above = moved(down, "tm", lambda i: i - 1)
    f32 = jnp.float32
    low = own[:2] + from_above[2:].astype(f32) + two_below.astype(f32)
    high = own[2:] + from_below[2:].astype(f32) + two_above.astype(f32)
    return jnp.concatenate([low, high], axis=0)[:, :LAGS]


def solution(mesh):
    return jax.shard_map(
        local,
        mesh=mesh,
        in_specs=(P("tm", "chan", None), P("chan", None), P("chan")),
        out_specs=P(("chan", "tm"), None, None),
        check_vma=False,
    )
```

```python
import functools
import math

import jax
import jax.numpy as jnp
import ml_dtypes
import numpy as np
from jax import lax
from jax.experimental import pallas as pl
from jax.experimental.pallas import tpu as pltpu
from jax.sharding import PartitionSpec as P

LAGS = 401
ROWS = 416
BLK = 16
SLOTS = 16
BINS = 256
LEFT = 64
BAND = 176
CHUNKS = (32, 16, 16)
PITCH = 513

water_share = 0.1
tiny_eps = 1e-06

MIB = 1024 * 1024


def make_tables(segments):
    length = 2 * BINS
    index = np.arange(BINS, dtype=np.int32)
    scale = np.float32(2.0 * math.pi / length)
    radians = (index[:, None] * index[None, :] % length).astype(np.float32) * scale
    forward = np.concatenate([np.cos(radians), -np.sin(radians)], axis=1)
    lag_shift = np.arange(LAGS, dtype=np.int32)[:, None] - (LAGS - 1) // 2
    lag_radians = (lag_shift * index[None, :] % length).astype(np.float32) * scale
    weight = np.where(index == 0, 1.0, 2.0).astype(np.float32)[None, :] / np.float32(
        math.sqrt(float(BINS * segments))
    )
    backward = np.concatenate([np.cos(lag_radians) * weight, -np.sin(lag_radians) * weight], axis=1)
    backward = np.pad(backward.astype(np.float32), ((0, ROWS - LAGS), (0, 0)))
    high = backward.astype(ml_dtypes.bfloat16)
    low = (backward - high.astype(np.float32)).astype(ml_dtypes.bfloat16)
    stacked = np.concatenate([high, low], axis=0)
    return (np.ascontiguousarray(forward.astype(ml_dtypes.bfloat16).T), stacked)


def whiten_tile(spec, lanes, put):
    total = jnp.zeros((8, 128), jnp.float32)
    for f in range(0, BINS, 8):
        real_part = spec[f:f + 8, lanes]
        imag_part = spec[BINS + f:BINS + f + 8, lanes]
        total = total + (real_part * real_part + imag_part * imag_part)
    level = jnp.sum(total, axis=0, keepdims=True) * (1.0 / BINS)
    floor = jnp.broadcast_to(water_share * level + tiny_eps, (8, 128))
    for f in range(0, BINS, 8):
        real_part = spec[f:f + 8, lanes]
        imag_part = spec[BINS + f:BINS + f + 8, lanes]
        inverse = lax.rsqrt(real_part * real_part + imag_part * imag_part + floor)
        put(f, real_part * inverse, imag_part * inverse)


def in_turns(count, transform, whiten, spec_a, spec_b):
    transform(0, spec_a)

    @pl.loop(0, count // 2)
    def _(pair):
        i = 2 * pair
        transform(i + 1, spec_b)
        whiten(i, spec_a)
        transform(jnp.minimum(i + 2, count - 1), spec_a)
        whiten(i + 1, spec_b)


def whiten_kernel(right_ref, odd_ref, table_ref, x0, b0, a1, b1, a2, b2, o5, out_ref,
                  band, spec_a, spec_b, bins_ref):
    segs = x0.shape[0]
    depth = 2 * segs
    pitch = depth + 1
    odd = odd_ref[0] == 1

    @pl.loop(0, segs)
    def _(s):
        band[s, 0:32, :] = x0[s]
        band[s, 32:64, :] = jnp.where(odd, b1[s], b0[s])
        band[s, 64:96, :] = a1[s]
        band[s, 96:128, :] = jnp.where(odd, b2[s], b1[s])
        band[s, 128:160, :] = a2[s]
        band[s, 160:176, :] = o5[s]

    starts = [pl.multiple_of(right_ref[q] * BLK, BLK) for q in range(SLOTS)]

    def transform(s, spec):
        rows = [band[s, pl.ds(start, BLK), :] for start in starts]
        spec[...] = lax.dot_general(
            table_ref[...],
            jnp.concatenate(rows, axis=0),
            (((1,), (1,)), ((), ())),
            preferred_element_type=jnp.float32,
        )

    def whiten(s, spec):
        for h in range(2):
            def put(f, real_part, imag_part):
                bins_ref[h, pl.ds(f * pitch + s, 8, stride=pitch), :] = real_part
                bins_ref[h, pl.ds(f * pitch + segs + s, 8, stride=pitch), :] = imag_part

            whiten_tile(spec, slice(h * 128, (h + 1) * 128), put)

    in_turns(segs, transform, whiten, spec_a, spec_b)

    @pl.loop(0, BINS // 4)
    def _(group):
        for step in range(4):
            f = group * 4 + step
            for h in range(2):
                out_ref[h, f] = bins_ref[h, pl.ds(f * pitch, depth), :].astype(jnp.bfloat16)


def whole(shape):
    return pl.BlockSpec(shape, lambda *_: (0,) * len(shape))


def whiten_bins(right, odd, table, whole_pieces, pieces, segs, offset):
    smem = pl.BlockSpec(memory_space=pltpu.SMEM)
    share = pl.BlockSpec((segs, 32, BINS), lambda _: (offset // segs, 0, 0))
    shape = (2, BINS, 2 * segs, 128)
    return pl.pallas_call(
        whiten_kernel,
        grid=(1,),
        out_shape=jax.ShapeDtypeStruct(shape, jnp.bfloat16),
        in_specs=[smem, smem, whole(table.shape), share, share] + [whole(p.shape) for p in pieces],
        out_specs=whole(shape),
        scratch_shapes=[
            pltpu.VMEM((segs, BAND, BINS), jnp.bfloat16),
            pltpu.VMEM((512, 256), jnp.float32),
            pltpu.VMEM((512, 256), jnp.float32),
            pltpu.VMEM((2, BINS * (2 * segs + 1), 128), jnp.float32),
        ],
        compiler_params=pltpu.CompilerParams(vmem_limit_bytes=(52 if segs > 16 else 32) * MIB),
        cost_estimate=pl.CostEstimate(flops=240_000_000 * segs, bytes_accessed=8_000_000, transcendentals=0),
        name="whiten",
    )(right, odd, table, *whole_pieces, *pieces)


def left_kernel(odd_ref, table_ref, x0, b0, *refs):
    pieces = refs[:len(CHUNKS)]
    out_ref, records, spec_a, spec_b, bins_ref = refs[len(CHUNKS):]
    odd = odd_ref[0] == 1
    segs = x0.shape[0]
    spread = LEFT + 1
    pitch = 2 * LEFT + 1
    offset = 0
    for piece in pieces:
        @pl.loop(0, piece.shape[0])
        def _(i, piece=piece, offset=offset):
            s = offset + i
            both = jnp.concatenate([x0[s], jnp.where(odd, piece[i], b0[s])], axis=0).astype(jnp.float32)
            for h in range(2):
                records[h, pl.ds(s * spread, LEFT), :] = both[:, h * 128:(h + 1) * 128]

        offset += piece.shape[0]

    def transform(quad, spec):
        rows = [
            jnp.concatenate([records[h, pl.ds(quad * 4 + k, segs, stride=spread), :] for h in range(2)], axis=1)
            for k in range(4)
        ]
        spec[...] = lax.dot_general(
            table_ref[...],
            jnp.concatenate(rows, axis=0).astype(jnp.bfloat16),
            (((1,), (1,)), ((), ())),
            preferred_element_type=jnp.float32,
        )

    in_first = lax.broadcasted_iota(jnp.int32, (8, 128), 1) < LEFT

    def whiten(quad, spec):
        for h in range(2):
            a = quad * 4 + 2 * h

            def put(f, real_part, imag_part):
                real_other = pltpu.roll(real_part, LEFT, 1)
                imag_other = pltpu.roll(imag_part, LEFT, 1)
                rows = [
                    (a, jnp.where(in_first, real_part, imag_other)),
                    (LEFT + a, jnp.where(in_first, imag_part, -real_other)),
                    (a + 1, jnp.where(in_first, real_other, imag_part)),
                    (LEFT + a + 1, jnp.where(in_first, imag_other, -real_part)),
                ]
                for row, value in rows:
                    bins_ref[pl.ds(f * pitch + row, 8, stride=pitch), :] = value

            whiten_tile(spec, slice(h * 128, (h + 1) * 128), put)

    in_turns(LEFT // 4, transform, whiten, spec_a, spec_b)

    @pl.loop(0, BINS // 4)
    def _(group):
        for step in range(4):
            f = group * 4 + step
            out_ref[f] = bins_ref[pl.ds(f * pitch, 2 * LEFT), :].astype(jnp.bfloat16)


def left_bins(odd, table, x0, b0, pieces):
    vmem = pl.BlockSpec(memory_space=pltpu.VMEM)
    smem = pl.BlockSpec(memory_space=pltpu.SMEM)
    return pl.pallas_call(
        left_kernel,
        out_shape=jax.ShapeDtypeStruct((BINS, 2 * LEFT, 128), jnp.bfloat16),
        in_specs=[smem] + [vmem] * (3 + len(pieces)),
        out_specs=vmem,
        scratch_shapes=[
            pltpu.VMEM((2, x0.shape[0] * (LEFT + 1), 128), jnp.float32),
            pltpu.VMEM((512, 256), jnp.float32),
            pltpu.VMEM((512, 256), jnp.float32),
            pltpu.VMEM((BINS * (2 * LEFT + 1), 128), jnp.float32),
        ],
        compiler_params=pltpu.CompilerParams(vmem_limit_bytes=48 * MIB),
        cost_estimate=pl.CostEstimate(flops=6_000_000_000, bytes_accessed=14_000_000, transcendentals=0),
        name="left",
    )(odd, table, x0, b0, *pieces)


def lag_sums(table_ref, cross_ref, lags):
    @pl.loop(0, BLK // 2)
    def _(pair):
        a = 2 * pair
        cross = jnp.concatenate(
            [cross_ref[pl.ds((a + k) * PITCH, 512), :].astype(jnp.bfloat16) for k in range(2)], axis=1
        )
        both = jnp.dot(table_ref[...], cross, preferred_element_type=jnp.float32)
        both = both[:ROWS] + both[ROWS:]
        lags[a] = both[:, :128]
        lags[a + 1] = both[:, 128:]


def by_slot(lags, put):
    block = lax.broadcasted_iota(jnp.int32, (BLK, 128), 1) // BLK
    odd_block = {d: (block // d) % 2 == 1 for d in (4, 2, 1)}

    @pl.loop(0, ROWS // BLK)
    def _(tile):
        rows = pl.ds(pl.multiple_of(tile * BLK, BLK), BLK)
        for ha in range(2):
            arrays = [lags[8 * ha + k, rows, :] for k in range(8)]
            for d in (4, 2, 1):
                for k in range(8):
                    if k & d == 0:
                        one, two = arrays[k], arrays[k + d]
                        arrays[k] = jnp.where(odd_block[d], pltpu.roll(two, BLK * d, 1), one)
                        arrays[k + d] = jnp.where(odd_block[d], two, pltpu.roll(one, 128 - BLK * d, 1))
            for k in range(8):
                put(k, rows, slice(ha * 128, (ha + 1) * 128), arrays[k])


def gram_kernel(tile, live_ref, first_ref, table_ref, left_ref, *refs):
    parts = refs[:len(CHUNKS)]
    outs = refs[len(CHUNKS):-2]
    sums, lags = refs[-2:]
    block = pl.program_id(0)
    bins = left_ref.shape[0]
    first = first_ref[...]
    chosen = [jnp.broadcast_to(first == i, (BLK, 128)) for i in range(3)]

    @pl.loop(0, bins // 4)
    def _(group):
        for step in range(4):
            local_bin = group * 4 + step
            f = block * bins + local_bin
            right = jnp.concatenate(
                [p[0, local_bin, part * n:(part + 1) * n, :] for part in range(2) for p, n in zip(parts, CHUNKS)],
                axis=0,
            )
            cross = jnp.dot(left_ref[local_bin], right, preferred_element_type=jnp.float32)
            for part in range(2):
                blocks = [cross[part * LEFT + i * BLK:part * LEFT + (i + 1) * BLK] for i in range(4)]
                own = blocks[3]
                for i in range(3):
                    own = jnp.where(chosen[i], blocks[i], own)
                for a in range(0, BLK, 8):
                    sums[pl.ds(a * PITCH + part * BINS + f, 8, stride=PITCH), :] = own[a:a + 8]

    @pl.when(block == pl.num_programs(0) - 1)
    def _():
        lag_sums(table_ref, sums, lags)
        live = [live_ref[8 * tile + q] == 1 for q in range(8)]

        def put(q, rows, lanes, value):
            value = jnp.where(live[q], value, 0.0)
            for out in outs:
                if q < out.shape[0]:
                    out[q, rows, lanes] = value.astype(out.dtype)
                    return
                q -= out.shape[0]

        by_slot(lags, put)


def gram(tile, live, first, table, left, parts, counts, dtype):
    step = 32
    shapes = [(n, ROWS, 256) for n in counts]
    return pl.pallas_call(
        functools.partial(gram_kernel, tile),
        grid=(BINS // step,),
        out_shape=[jax.ShapeDtypeStruct(s, dtype) for s in shapes],
        in_specs=[
            pl.BlockSpec(memory_space=pltpu.SMEM),
            pl.BlockSpec((1, 128), lambda k: (0, tile)),
            whole(table.shape),
            pl.BlockSpec((step,) + left.shape[1:], lambda k: (k, 0, 0)),
        ]
        + [pl.BlockSpec((1, step) + p.shape[2:], lambda k: (tile, k, 0, 0)) for p in parts],
        out_specs=[whole(s) for s in shapes],
        scratch_shapes=[
            pltpu.VMEM((BLK * PITCH, 128), jnp.float32),
            pltpu.VMEM((BLK, ROWS, 128), jnp.float32),
        ],
        compiler_params=pltpu.CompilerParams(vmem_limit_bytes=32 * MIB),
        cost_estimate=pl.CostEstimate(flops=16_000_000_000, bytes_accessed=20_000_000, transcendentals=0),
        name="gram",
    )(live, first, table, left, *parts)


def moved(block, axis, to):
    size = lax.axis_size(axis)
    return lax.ppermute(block, axis, [(i, to(i) % size) for i in range(size)])


def one_chip(block):
    return moved(block, "chan", lambda i: i - 2)


def swap(block):
    return moved(block, "chan", lambda i: i ^ 1)


def first_half(block, distance):
    return moved(block[:, :BLK], "chan", lambda i: i - distance)


def local(records, pair_blocks, pair_counts):
    segs = records.shape[0]
    table, backward = make_tables(segs * lax.axis_size("tm"))
    owner = lax.axis_index("chan")
    row = lax.axis_index("tm")

    group = np.array([2, 2, 1, 1, 2, 2, 3, 3, 1, 1, 3, 3, 0, 0, 0, 0], np.int32)
    inside = np.array([0, 1, 2, 3, 2, 3, 0, 1, 0, 1, 2, 3, 0, 1, 2, 3], np.int32)
    order = (row + group) % 4 * 4 + inside
    relative = pair_blocks[order] - 2 * owner
    first = jnp.clip(relative[:, 0], 0, 3)
    right = jnp.clip(relative[:, 1], 0, 10)
    live = (order < pair_counts[0]).astype(jnp.int32)
    odd = (owner % 2).astype(jnp.int32)[None]
    first_lanes = jnp.repeat(first, BLK)[None, :]

    barrier = lax.optimization_barrier
    starts = np.cumsum((0,) + CHUNKS)
    x = [records[starts[c]:starts[c + 1]] for c in range(len(CHUNKS))]

    def whitened(c, *pieces):
        return whiten_bins(right, odd, table, [records, b0], pieces, CHUNKS[c], int(starts[c]))

    a1_0, b0 = one_chip(x[0]), swap(records)
    x[1], a1_0 = barrier((x[1], a1_0))
    a2_0, b1_0, a1_1 = one_chip(a1_0), swap(a1_0), one_chip(x[1])
    x[2], a1_1 = barrier((x[2], a1_1))
    b2_0, o5_0, a2_1, b1_1, a1_2 = swap(a2_0), first_half(a2_0, 1), one_chip(a1_1), swap(a1_1), one_chip(x[2])
    part_0 = whitened(0, a1_0, b1_0, a2_0, b2_0, o5_0)
    a2_1, a1_2, part_0 = barrier((a2_1, a1_2, part_0))
    b2_1, o5_1 = swap(a2_1), first_half(a2_1, 1)
    a2_2, b1_2, o5_2 = one_chip(a1_2), swap(a1_2), first_half(a1_2, 3)
    left = left_bins(odd, table, records, b0, [b1_0, b1_1, b1_2])
    part_1 = whitened(1, a1_1, b1_1, a2_1, b2_1, o5_1)
    a2_2, o5_2, left, part_1 = barrier((a2_2, o5_2, left, part_1))
    b2_2 = swap(a2_2)
    part_2 = whitened(2, a1_2, b1_2, a2_2, b2_2, o5_2)

    parts = [part_0, part_1, part_2]
    plus, minus = gram(0, live, first_lanes, backward, left, parts, (4, 4), jnp.bfloat16)
    keep, other, own = gram(1, live, first_lanes, backward, left, parts, (2, 2, 4), jnp.float32)

    from_below = moved(plus, "tm", lambda i: i + 1)
    from_above = moved(minus, "tm", lambda i: i - 1)
    up = (keep + from_below[:2].astype(jnp.float32)).astype(jnp.bfloat16)
    down = (other + from_above[:2].astype(jnp.float32)).astype(jnp.bfloat16)
    two_below = moved(up, "tm", lambda i: i + 1)
    two_above = moved(down, "tm", lambda i: i - 1)
    f32 = jnp.float32
    low = own[:2] + from_above[2:].astype(f32) + two_below.astype(f32)
    high = own[2:] + from_below[2:].astype(f32) + two_above.astype(f32)
    return jnp.concatenate([low, high], axis=0)[:, :LAGS]


def solution(mesh):
    return jax.shard_map(
        local,
        mesh=mesh,
        in_specs=(P("tm", "chan", None), P("chan", None), P("chan")),
        out_specs=P(("chan", "tm"), None, None),
        check_vma=False,
    )
```

```python
import functools
import math

import jax
import jax.numpy as jnp
import ml_dtypes
import numpy as np
from jax import lax
from jax.experimental import pallas as pl
from jax.experimental.pallas import tpu as pltpu
from jax.sharding import PartitionSpec as P

LAGS = 401
HALF = 208
ROWS = 2 * HALF
BLK = 16
SLOTS = 16
BINS = 256
LEFT = 64
BAND = 176
CHUNKS = (32, 32)
PITCH = 513
GROUP = 16

water_share = 0.1
tiny_eps = 1e-06

MIB = 1024 * 1024


def make_tables(segments):
    length = 2 * BINS
    index = np.arange(BINS, dtype=np.int32)
    scale = np.float32(2.0 * math.pi / length)
    radians = (index[:, None] * index[None, :] % length).astype(np.float32) * scale
    forward = np.concatenate([np.cos(radians), -np.sin(radians)], axis=1)
    shift = np.arange(HALF, dtype=np.int32)[:, None]
    lag_radians = (shift * index[None, :] % length).astype(np.float32) * scale
    weight = np.where(index == 0, 1.0, 2.0).astype(np.float32)[None, :] / np.float32(
        math.sqrt(float(BINS * segments))
    )
    waves = np.stack([np.cos(lag_radians) * weight, -np.sin(lag_radians) * weight]).astype(np.float32)
    waves[:, LAGS // 2 + 1:] = 0.0
    high = waves.astype(ml_dtypes.bfloat16)
    low = (waves - high.astype(np.float32)).astype(ml_dtypes.bfloat16)
    return (np.ascontiguousarray(forward.astype(ml_dtypes.bfloat16).T), np.concatenate([high, low], axis=1))


def whiten_tile(spec, lanes, put):
    total = jnp.zeros((8, 128), jnp.float32)
    for f in range(0, BINS, 8):
        real_part = spec[f:f + 8, lanes]
        imag_part = spec[BINS + f:BINS + f + 8, lanes]
        total = total + (real_part * real_part + imag_part * imag_part)
    level = jnp.sum(total, axis=0, keepdims=True) * (1.0 / BINS)
    floor = jnp.broadcast_to(water_share * level + tiny_eps, (8, 128))
    for f in range(0, BINS, 8):
        real_part = spec[f:f + 8, lanes]
        imag_part = spec[BINS + f:BINS + f + 8, lanes]
        inverse = lax.rsqrt(real_part * real_part + imag_part * imag_part + floor)
        put(f, real_part * inverse, imag_part * inverse)


def in_turns(count, transform, whiten, spec_a, spec_b):
    transform(0, spec_a)

    @pl.loop(0, count // 2)
    def _(pair):
        i = 2 * pair
        transform(i + 1, spec_b)
        whiten(i, spec_a)
        transform(jnp.minimum(i + 2, count - 1), spec_a)
        whiten(i + 1, spec_b)


def whiten_kernel(right_ref, odd_ref, table_ref, x0, b0, a1, b1, a2, b2, o5, out_ref,
                  band, spec_a, spec_b, bins_ref, packed, sems):
    segs = x0.shape[0]
    depth = 2 * segs
    pitch = depth + 1
    odd = odd_ref[0] == 1

    @pl.loop(0, segs)
    def _(s):
        band[s, 0:32, :] = x0[s]
        band[s, 32:64, :] = jnp.where(odd, b1[s], b0[s])
        band[s, 64:96, :] = a1[s]
        band[s, 96:128, :] = jnp.where(odd, b2[s], b1[s])
        band[s, 128:160, :] = a2[s]
        band[s, 160:176, :] = o5[s]

    starts = [pl.multiple_of(right_ref[q] * BLK, BLK) for q in range(SLOTS)]

    def transform(s, spec):
        rows = [band[s, pl.ds(start, BLK), :] for start in starts]
        spec[...] = lax.dot_general(
            table_ref[...],
            jnp.concatenate(rows, axis=0),
            (((1,), (1,)), ((), ())),
            preferred_element_type=jnp.float32,
        )

    def whiten(s, spec):
        for h in range(2):
            def put(f, real_part, imag_part):
                bins_ref[h, pl.ds(f * pitch + s, 8, stride=pitch), :] = real_part
                bins_ref[h, pl.ds(f * pitch + segs + s, 8, stride=pitch), :] = imag_part

            whiten_tile(spec, slice(h * 128, (h + 1) * 128), put)

    in_turns(segs, transform, whiten, spec_a, spec_b)

    def copy(group):
        some = pl.ds(group * GROUP, GROUP)
        return pltpu.make_async_copy(packed.at[:, some], out_ref.at[:, some], sems.at[group])

    @pl.loop(0, BINS // GROUP)
    def _(group):
        for step in range(GROUP):
            f = group * GROUP + step
            for h in range(2):
                packed[h, f] = bins_ref[h, pl.ds(f * pitch, depth), :].astype(jnp.bfloat16)
        copy(group).start()

    @pl.loop(0, BINS // GROUP)
    def _(group):
        copy(group).wait()


def whole(shape):
    return pl.BlockSpec(shape, lambda *_: (0,) * len(shape))


def whiten_bins(right, odd, table, whole_pieces, pieces, segs, offset):
    smem = pl.BlockSpec(memory_space=pltpu.SMEM)
    share = pl.BlockSpec((segs, 32, BINS), lambda _: (offset // segs, 0, 0))
    shape = (2, BINS, 2 * segs, 128)
    return pl.pallas_call(
        whiten_kernel,
        grid=(1,),
        out_shape=jax.ShapeDtypeStruct(shape, jnp.bfloat16),
        in_specs=[smem, smem, whole(table.shape), share, share] + [whole(p.shape) for p in pieces],
        out_specs=pl.BlockSpec(memory_space=pl.ANY),
        scratch_shapes=[
            pltpu.VMEM((segs, BAND, BINS), jnp.bfloat16),
            pltpu.VMEM((512, 256), jnp.float32),
            pltpu.VMEM((512, 256), jnp.float32),
            pltpu.VMEM((2, BINS * (2 * segs + 1), 128), jnp.float32),
            pltpu.VMEM(shape, jnp.bfloat16),
            pltpu.SemaphoreType.DMA((BINS // GROUP,)),
        ],
        compiler_params=pltpu.CompilerParams(vmem_limit_bytes=52 * MIB),
        cost_estimate=pl.CostEstimate(flops=240_000_000 * segs, bytes_accessed=8_000_000, transcendentals=0),
        name="whiten",
    )(right, odd, table, *whole_pieces, *pieces)


def left_kernel(odd_ref, table_ref, x0, b0, *refs):
    pieces = refs[:len(CHUNKS)]
    out_ref, records, spec_a, spec_b, bins_ref, packed, sems = refs[len(CHUNKS):]
    odd = odd_ref[0] == 1
    segs = x0.shape[0]
    spread = LEFT + 1
    pitch = 2 * LEFT + 1
    offset = 0
    for piece in pieces:
        @pl.loop(0, piece.shape[0])
        def _(i, piece=piece, offset=offset):
            s = offset + i
            both = jnp.concatenate([x0[s], jnp.where(odd, piece[i], b0[s])], axis=0).astype(jnp.float32)
            for h in range(2):
                records[h, pl.ds(s * spread, LEFT), :] = both[:, h * 128:(h + 1) * 128]

        offset += piece.shape[0]

    def transform(quad, spec):
        rows = [
            jnp.concatenate([records[h, pl.ds(quad * 4 + k, segs, stride=spread), :] for h in range(2)], axis=1)
            for k in range(4)
        ]
        spec[...] = lax.dot_general(
            table_ref[...],
            jnp.concatenate(rows, axis=0).astype(jnp.bfloat16),
            (((1,), (1,)), ((), ())),
            preferred_element_type=jnp.float32,
        )

    in_first = lax.broadcasted_iota(jnp.int32, (8, 128), 1) < LEFT

    def whiten(quad, spec):
        for h in range(2):
            a = quad * 4 + 2 * h

            def put(f, real_part, imag_part):
                real_other = pltpu.roll(real_part, LEFT, 1)
                imag_other = pltpu.roll(imag_part, LEFT, 1)
                rows = [
                    (a, jnp.where(in_first, real_part, imag_other)),
                    (LEFT + a, jnp.where(in_first, imag_part, -real_other)),
                    (a + 1, jnp.where(in_first, real_other, imag_part)),
                    (LEFT + a + 1, jnp.where(in_first, imag_other, -real_part)),
                ]
                for row, value in rows:
                    bins_ref[pl.ds(f * pitch + row, 8, stride=pitch), :] = value

            whiten_tile(spec, slice(h * 128, (h + 1) * 128), put)

    in_turns(LEFT // 4, transform, whiten, spec_a, spec_b)

    def copy(group):
        some = pl.ds(group * GROUP, GROUP)
        return pltpu.make_async_copy(packed.at[some], out_ref.at[some], sems.at[group])

    @pl.loop(0, BINS // GROUP)
    def _(group):
        for step in range(GROUP):
            f = group * GROUP + step
            packed[f] = bins_ref[pl.ds(f * pitch, 2 * LEFT), :].astype(jnp.bfloat16)
        copy(group).start()

    @pl.loop(0, BINS // GROUP)
    def _(group):
        copy(group).wait()


def left_bins(odd, table, x0, b0, pieces):
    vmem = pl.BlockSpec(memory_space=pltpu.VMEM)
    smem = pl.BlockSpec(memory_space=pltpu.SMEM)
    return pl.pallas_call(
        left_kernel,
        out_shape=jax.ShapeDtypeStruct((BINS, 2 * LEFT, 128), jnp.bfloat16),
        in_specs=[smem] + [vmem] * (3 + len(pieces)),
        out_specs=pl.BlockSpec(memory_space=pl.ANY),
        scratch_shapes=[
            pltpu.VMEM((2, x0.shape[0] * (LEFT + 1), 128), jnp.float32),
            pltpu.VMEM((512, 256), jnp.float32),
            pltpu.VMEM((512, 256), jnp.float32),
            pltpu.VMEM((BINS * (2 * LEFT + 1), 128), jnp.float32),
            pltpu.VMEM((BINS, 2 * LEFT, 128), jnp.bfloat16),
            pltpu.SemaphoreType.DMA((BINS // GROUP,)),
        ],
        compiler_params=pltpu.CompilerParams(vmem_limit_bytes=52 * MIB),
        cost_estimate=pl.CostEstimate(flops=6_000_000_000, bytes_accessed=14_000_000, transcendentals=0),
        name="left",
    )(odd, table, x0, b0, *pieces)


def lag_sums(table_ref, cross_ref, lags):
    @pl.loop(0, BLK // 4)
    def _(four):
        for a in (4 * four, 4 * four + 2):
            for part in range(2):
                cross = jnp.concatenate(
                    [
                        cross_ref[pl.ds((a + k) * PITCH + part * BINS, BINS), :].astype(jnp.bfloat16)
                        for k in range(2)
                    ],
                    axis=1,
                )
                both = jnp.dot(table_ref[part], cross, preferred_element_type=jnp.float32)
                both = both[:HALF] + both[HALF:]
                lags[a, part * HALF:(part + 1) * HALF, :] = both[:, :128]
                lags[a + 1, part * HALF:(part + 1) * HALF, :] = both[:, 128:]


def by_slot(lags, put):
    block = lax.broadcasted_iota(jnp.int32, (BLK, 128), 1) // BLK
    odd_block = {d: (block // d) % 2 == 1 for d in (4, 2, 1)}

    @pl.loop(0, ROWS // (2 * BLK))
    def _(tile):
        for sub in range(2):
            rows = pl.ds(pl.multiple_of((2 * tile + sub) * BLK, BLK), BLK)
            for ha in range(2):
                arrays = [lags[8 * ha + k, rows, :] for k in range(8)]
                for d in (4, 2, 1):
                    for k in range(8):
                        if k & d == 0:
                            one, two = arrays[k], arrays[k + d]
                            arrays[k] = jnp.where(odd_block[d], pltpu.roll(two, BLK * d, 1), one)
                            arrays[k + d] = jnp.where(odd_block[d], two, pltpu.roll(one, 128 - BLK * d, 1))
                for k in range(8):
                    put(k, rows, slice(ha * 128, (ha + 1) * 128), arrays[k])


def gram_kernel(tile, live_ref, first_ref, table_ref, left_ref, *refs):
    parts = refs[:len(CHUNKS)]
    outs = refs[len(CHUNKS):-2]
    sums, lags = refs[-2:]
    block = pl.program_id(0)
    bins = left_ref.shape[0]
    first = first_ref[...]
    chosen = [jnp.broadcast_to(first == i, (BLK, 128)) for i in range(3)]

    @pl.loop(0, bins // GROUP)
    def _(group):
        for step in range(GROUP):
            local_bin = group * GROUP + step
            f = block * bins + local_bin
            right = jnp.concatenate(
                [p[0, local_bin, part * n:(part + 1) * n, :] for part in range(2) for p, n in zip(parts, CHUNKS)],
                axis=0,
            )
            cross = jnp.dot(left_ref[local_bin], right, preferred_element_type=jnp.float32)
            for part in range(2):
                blocks = [cross[part * LEFT + i * BLK:part * LEFT + (i + 1) * BLK] for i in range(4)]
                own = blocks[3]
                for i in range(3):
                    own = jnp.where(chosen[i], blocks[i], own)
                for a in range(0, BLK, 8):
                    sums[pl.ds(a * PITCH + part * BINS + f, 8, stride=PITCH), :] = own[a:a + 8]

    @pl.when(block == pl.num_programs(0) - 1)
    def _():
        lag_sums(table_ref, sums, lags)
        live = [live_ref[8 * tile + q] == 1 for q in range(8)]

        def put(q, rows, lanes, value):
            value = jnp.where(live[q], value, 0.0)
            for out in outs:
                if q < out.shape[0]:
                    out[q, rows, lanes] = value.astype(out.dtype)
                    return
                q -= out.shape[0]

        by_slot(lags, put)


def gram(tile, live, first, table, left, parts, counts, dtype):
    step = 32
    shapes = [(n, ROWS, 256) for n in counts]
    return pl.pallas_call(
        functools.partial(gram_kernel, tile),
        grid=(BINS // step,),
        out_shape=[jax.ShapeDtypeStruct(s, dtype) for s in shapes],
        in_specs=[
            pl.BlockSpec(memory_space=pltpu.SMEM),
            pl.BlockSpec((1, 128), lambda k: (0, tile)),
            whole(table.shape),
            pl.BlockSpec((step,) + left.shape[1:], lambda k: (k, 0, 0)),
        ]
        + [pl.BlockSpec((1, step) + p.shape[2:], lambda k: (tile, k, 0, 0)) for p in parts],
        out_specs=[whole(s) for s in shapes],
        scratch_shapes=[
            pltpu.VMEM((BLK * PITCH, 128), jnp.float32),
            pltpu.VMEM((BLK, ROWS, 128), jnp.float32),
        ],
        compiler_params=pltpu.CompilerParams(vmem_limit_bytes=48 * MIB),
        cost_estimate=pl.CostEstimate(flops=16_000_000_000, bytes_accessed=20_000_000, transcendentals=0),
        name="gram",
    )(live, first, table, left, *parts)


def final_kernel(own, below, above, two_below, two_above, out):
    row = lax.broadcasted_iota(jnp.int32, (8, 256), 0)

    def reversed_rows(x):
        x = pltpu.roll(x, 4, 0)
        x = jnp.where((row & 2) == 2, pltpu.roll(x, 2, 0), pltpu.roll(x, 6, 0))
        return jnp.where((row & 1) == 1, pltpu.roll(x, 1, 0), pltpu.roll(x, 7, 0))

    middle = LAGS // 2
    for pair, (near, far) in enumerate(((above, two_below), (below, two_above))):
        @pl.loop(0, 2)
        def _(k, pair=pair, near=near, far=far):
            q = 2 * pair + k
            for start in range(0, HALF, BLK):
                even, odd = (
                    own[q, rows, :] + near[2 + k, rows, :].astype(jnp.float32) + far[k, rows, :].astype(jnp.float32)
                    for rows in (slice(start, start + BLK), slice(HALF + start, HALF + start + BLK))
                )
                later, earlier = even + odd, even - odd
                for u in range(start, start + BLK, 8):
                    n = min(8, middle + 1 - u)
                    if n > 0:
                        out[q, middle + u:middle + u + n, :] = later[u - start:u - start + n]
                        turned = reversed_rows(earlier[u - start:u - start + 8])
                        out[q, middle - u - n + 1:middle - u + 1, :] = turned[8 - n:]


def final(own, below, above, two_below, two_above):
    vmem = pl.BlockSpec(memory_space=pltpu.VMEM)
    return pl.pallas_call(
        final_kernel,
        out_shape=jax.ShapeDtypeStruct((4, LAGS, 256), jnp.float32),
        in_specs=[vmem] * 5,
        out_specs=vmem,
        cost_estimate=pl.CostEstimate(flops=10_000_000, bytes_accessed=7_000_000, transcendentals=0),
        name="final",
    )(own, below, above, two_below, two_above)


def moved(block, axis, to):
    size = lax.axis_size(axis)
    return lax.ppermute(block, axis, [(i, to(i) % size) for i in range(size)])


def one_chip(block):
    return moved(block, "chan", lambda i: i - 2)


def swap(block):
    return moved(block, "chan", lambda i: i ^ 1)


def first_half(block, distance):
    return moved(block[:, :BLK], "chan", lambda i: i - distance)


def local(records, pair_blocks, pair_counts):
    segs = records.shape[0]
    table, backward = make_tables(segs * lax.axis_size("tm"))
    owner = lax.axis_index("chan")
    row = lax.axis_index("tm")

    group = np.array([2, 2, 1, 1, 2, 2, 3, 3, 1, 1, 3, 3, 0, 0, 0, 0], np.int32)
    inside = np.array([0, 1, 2, 3, 2, 3, 0, 1, 0, 1, 2, 3, 0, 1, 2, 3], np.int32)
    order = (row + group) % 4 * 4 + inside
    relative = pair_blocks[order] - 2 * owner
    first = jnp.clip(relative[:, 0], 0, 3)
    right = jnp.clip(relative[:, 1], 0, 10)
    live = (order < pair_counts[0]).astype(jnp.int32)
    odd = (owner % 2).astype(jnp.int32)[None]
    first_lanes = jnp.repeat(first, BLK)[None, :]

    barrier = lax.optimization_barrier
    step = CHUNKS[0]
    x_0, x_1 = records[:step], records[step:]

    def whitened(c, *pieces):
        return whiten_bins(right, odd, table, [records, b0], pieces, step, c * step)

    a1_0, a1_1, b0 = one_chip(x_0), one_chip(x_1), swap(records)
    a2_0, b1_0 = one_chip(a1_0), swap(a1_0)
    a2_1, b1_1 = one_chip(a1_1), swap(a1_1)
    b2_0, o5_0 = swap(a2_0), first_half(a2_0, 1)
    part_0 = whitened(0, a1_0, b1_0, a2_0, b2_0, o5_0)
    a2_1, b1_1, part_0 = barrier((a2_1, b1_1, part_0))
    b2_1, o5_1 = swap(a2_1), first_half(a2_1, 1)
    left = left_bins(odd, table, records, b0, [b1_0, b1_1])
    part_1 = whitened(1, a1_1, b1_1, a2_1, b2_1, o5_1)

    parts = [part_0, part_1]
    plus, minus = gram(0, live, first_lanes, backward, left, parts, (4, 4), jnp.bfloat16)
    keep, other, own = gram(1, live, first_lanes, backward, left, parts, (2, 2, 4), jnp.float32)

    from_below = moved(plus, "tm", lambda i: i + 1)
    from_above = moved(minus, "tm", lambda i: i - 1)
    up = (keep + from_below[:2].astype(jnp.float32)).astype(jnp.bfloat16)
    down = (other + from_above[:2].astype(jnp.float32)).astype(jnp.bfloat16)
    two_below = moved(up, "tm", lambda i: i + 1)
    two_above = moved(down, "tm", lambda i: i - 1)
    return final(own, from_below, from_above, two_below, two_above)


def solution(mesh):
    return jax.shard_map(
        local,
        mesh=mesh,
        in_specs=(P("tm", "chan", None), P("chan", None), P("chan")),
        out_specs=P(("chan", "tm"), None, None),
        check_vma=False,
    )
```

```python
import functools
import math

import jax
import jax.numpy as jnp
import ml_dtypes
import numpy as np
from jax import lax
from jax.experimental import pallas as pl
from jax.experimental.pallas import tpu as pltpu
from jax.sharding import PartitionSpec as P

LAGS = 401
HALF = 208
ROWS = 2 * HALF
BLK = 16
SLOTS = 16
BINS = 256
LEFT = 64
BAND = 176
CHUNKS = (16, 48)
PITCH = 513
GROUP = 16

water_share = 0.1
tiny_eps = 1e-06

MIB = 1024 * 1024


def make_tables(segments):
    length = 2 * BINS
    index = np.arange(BINS, dtype=np.int32)
    scale = np.float32(2.0 * math.pi / length)
    radians = (index[:, None] * index[None, :] % length).astype(np.float32) * scale
    forward = np.concatenate([np.cos(radians), -np.sin(radians)], axis=1)
    shift = np.arange(HALF, dtype=np.int32)[:, None]
    lag_radians = (shift * index[None, :] % length).astype(np.float32) * scale
    weight = np.where(index == 0, 1.0, 2.0).astype(np.float32)[None, :] / np.float32(
        math.sqrt(float(BINS * segments))
    )
    waves = np.stack([np.cos(lag_radians) * weight, -np.sin(lag_radians) * weight]).astype(np.float32)
    waves[:, LAGS // 2 + 1:] = 0.0
    high = waves.astype(ml_dtypes.bfloat16)
    low = (waves - high.astype(np.float32)).astype(ml_dtypes.bfloat16)
    return (np.ascontiguousarray(forward.astype(ml_dtypes.bfloat16).T), np.concatenate([high, low], axis=1))


def whiten_tile(spec, lanes, put):
    total = jnp.zeros((8, 128), jnp.float32)
    for f in range(0, BINS, 8):
        real_part = spec[f:f + 8, lanes]
        imag_part = spec[BINS + f:BINS + f + 8, lanes]
        total = total + (real_part * real_part + imag_part * imag_part)
    level = jnp.sum(total, axis=0, keepdims=True) * (1.0 / BINS)
    floor = jnp.broadcast_to(water_share * level + tiny_eps, (8, 128))
    for f in range(0, BINS, 8):
        real_part = spec[f:f + 8, lanes]
        imag_part = spec[BINS + f:BINS + f + 8, lanes]
        inverse = lax.rsqrt(real_part * real_part + imag_part * imag_part + floor)
        put(f, real_part * inverse, imag_part * inverse)


def in_turns(count, transform, whiten, spec_a, spec_b):
    transform(0, spec_a)

    @pl.loop(0, count // 2)
    def _(pair):
        i = 2 * pair
        transform(i + 1, spec_b)
        whiten(i, spec_a)
        transform(jnp.minimum(i + 2, count - 1), spec_a)
        whiten(i + 1, spec_b)


def whiten_kernel(offset, right_ref, odd_ref, table_ref, x0, b0, a1, b1, a2, b2, o5, out_ref,
                  band, spec_a, spec_b, bins_ref, packed, sems):
    segs = a1.shape[0]
    depth = 2 * segs
    pitch = depth + 1
    odd = odd_ref[0] == 1

    @pl.loop(0, segs)
    def _(s):
        band[s, 0:32, :] = x0[offset + s]
        band[s, 32:64, :] = jnp.where(odd, b1[s], b0[offset + s])
        band[s, 64:96, :] = a1[s]
        band[s, 96:128, :] = jnp.where(odd, b2[s], b1[s])
        band[s, 128:160, :] = a2[s]
        band[s, 160:176, :] = o5[s]

    starts = [pl.multiple_of(right_ref[q] * BLK, BLK) for q in range(SLOTS)]

    def transform(s, spec):
        rows = [band[s, pl.ds(start, BLK), :] for start in starts]
        spec[...] = lax.dot_general(
            table_ref[...],
            jnp.concatenate(rows, axis=0),
            (((1,), (1,)), ((), ())),
            preferred_element_type=jnp.float32,
        )

    def whiten(s, spec):
        for h in range(2):
            def put(f, real_part, imag_part):
                bins_ref[h, pl.ds(f * pitch + s, 8, stride=pitch), :] = real_part
                bins_ref[h, pl.ds(f * pitch + segs + s, 8, stride=pitch), :] = imag_part

            whiten_tile(spec, slice(h * 128, (h + 1) * 128), put)

    in_turns(segs, transform, whiten, spec_a, spec_b)

    def copy(group):
        some = pl.ds(group * GROUP, GROUP)
        return pltpu.make_async_copy(packed.at[:, some], out_ref.at[:, some], sems.at[group])

    @pl.loop(0, BINS // GROUP)
    def _(group):
        for step in range(GROUP):
            f = group * GROUP + step
            for h in range(2):
                packed[h, f] = bins_ref[h, pl.ds(f * pitch, depth), :].astype(jnp.bfloat16)
        copy(group).start()

    @pl.loop(0, BINS // GROUP)
    def _(group):
        copy(group).wait()


def whole(shape):
    return pl.BlockSpec(shape, lambda *_: (0,) * len(shape))


def whiten_bins(right, odd, table, whole_pieces, pieces, offset):
    smem = pl.BlockSpec(memory_space=pltpu.SMEM)
    vmem = pl.BlockSpec(memory_space=pltpu.VMEM)
    segs = pieces[0].shape[0]
    shape = (2, BINS, 2 * segs, 128)
    return pl.pallas_call(
        functools.partial(whiten_kernel, offset),
        out_shape=jax.ShapeDtypeStruct(shape, jnp.bfloat16),
        in_specs=[smem, smem] + [vmem] * (3 + len(pieces)),
        out_specs=pl.BlockSpec(memory_space=pl.ANY),
        scratch_shapes=[
            pltpu.VMEM((segs, BAND, BINS), jnp.bfloat16),
            pltpu.VMEM((512, 256), jnp.float32),
            pltpu.VMEM((512, 256), jnp.float32),
            pltpu.VMEM((2, BINS * (2 * segs + 1), 128), jnp.float32),
            pltpu.VMEM(shape, jnp.bfloat16),
            pltpu.SemaphoreType.DMA((BINS // GROUP,)),
        ],
        compiler_params=pltpu.CompilerParams(vmem_limit_bytes=54 * MIB),
        cost_estimate=pl.CostEstimate(flops=240_000_000 * segs, bytes_accessed=8_000_000, transcendentals=0),
        name="whiten",
    )(right, odd, table, *whole_pieces, *pieces)


def left_kernel(odd_ref, table_ref, x0, b0, *refs):
    pieces = refs[:len(CHUNKS)]
    out_ref, records, spec_a, spec_b, bins_ref, packed, sems = refs[len(CHUNKS):]
    odd = odd_ref[0] == 1
    segs = x0.shape[0]
    spread = LEFT + 1
    pitch = 2 * LEFT + 1
    offset = 0
    for piece in pieces:
        @pl.loop(0, piece.shape[0])
        def _(i, piece=piece, offset=offset):
            s = offset + i
            both = jnp.concatenate([x0[s], jnp.where(odd, piece[i], b0[s])], axis=0).astype(jnp.float32)
            for h in range(2):
                records[h, pl.ds(s * spread, LEFT), :] = both[:, h * 128:(h + 1) * 128]

        offset += piece.shape[0]

    def transform(quad, spec):
        rows = [
            jnp.concatenate([records[h, pl.ds(quad * 4 + k, segs, stride=spread), :] for h in range(2)], axis=1)
            for k in range(4)
        ]
        spec[...] = lax.dot_general(
            table_ref[...],
            jnp.concatenate(rows, axis=0).astype(jnp.bfloat16),
            (((1,), (1,)), ((), ())),
            preferred_element_type=jnp.float32,
        )

    in_first = lax.broadcasted_iota(jnp.int32, (8, 128), 1) < LEFT

    def whiten(quad, spec):
        for h in range(2):
            a = quad * 4 + 2 * h

            def put(f, real_part, imag_part):
                real_other = pltpu.roll(real_part, LEFT, 1)
                imag_other = pltpu.roll(imag_part, LEFT, 1)
                rows = [
                    (a, jnp.where(in_first, real_part, imag_other)),
                    (LEFT + a, jnp.where(in_first, imag_part, -real_other)),
                    (a + 1, jnp.where(in_first, real_other, imag_part)),
                    (LEFT + a + 1, jnp.where(in_first, imag_other, -real_part)),
                ]
                for row, value in rows:
                    bins_ref[pl.ds(f * pitch + row, 8, stride=pitch), :] = value

            whiten_tile(spec, slice(h * 128, (h + 1) * 128), put)

    in_turns(LEFT // 4, transform, whiten, spec_a, spec_b)

    def copy(group):
        some = pl.ds(group * GROUP, GROUP)
        return pltpu.make_async_copy(packed.at[some], out_ref.at[some], sems.at[group])

    @pl.loop(0, BINS // GROUP)
    def _(group):
        for step in range(GROUP):
            f = group * GROUP + step
            packed[f] = bins_ref[pl.ds(f * pitch, 2 * LEFT), :].astype(jnp.bfloat16)
        copy(group).start()

    @pl.loop(0, BINS // GROUP)
    def _(group):
        copy(group).wait()


def left_bins(odd, table, x0, b0, pieces):
    vmem = pl.BlockSpec(memory_space=pltpu.VMEM)
    smem = pl.BlockSpec(memory_space=pltpu.SMEM)
    return pl.pallas_call(
        left_kernel,
        out_shape=jax.ShapeDtypeStruct((BINS, 2 * LEFT, 128), jnp.bfloat16),
        in_specs=[smem] + [vmem] * (3 + len(pieces)),
        out_specs=pl.BlockSpec(memory_space=pl.ANY),
        scratch_shapes=[
            pltpu.VMEM((2, x0.shape[0] * (LEFT + 1), 128), jnp.float32),
            pltpu.VMEM((512, 256), jnp.float32),
            pltpu.VMEM((512, 256), jnp.float32),
            pltpu.VMEM((BINS * (2 * LEFT + 1), 128), jnp.float32),
            pltpu.VMEM((BINS, 2 * LEFT, 128), jnp.bfloat16),
            pltpu.SemaphoreType.DMA((BINS // GROUP,)),
        ],
        compiler_params=pltpu.CompilerParams(vmem_limit_bytes=52 * MIB),
        cost_estimate=pl.CostEstimate(flops=6_000_000_000, bytes_accessed=14_000_000, transcendentals=0),
        name="left",
    )(odd, table, x0, b0, *pieces)


def lag_sums(table_ref, cross_ref, lags):
    @pl.loop(0, BLK // 8)
    def _(eight):
        for pair in range(4):
            a = 8 * eight + 2 * pair
            for part in range(2):
                cross = jnp.concatenate(
                    [
                        cross_ref[pl.ds((a + k) * PITCH + part * BINS, BINS), :].astype(jnp.bfloat16)
                        for k in range(2)
                    ],
                    axis=1,
                )
                both = jnp.dot(table_ref[part], cross, preferred_element_type=jnp.float32)
                both = both[:HALF] + both[HALF:]
                lags[a, part * HALF:(part + 1) * HALF, :] = both[:, :128]
                lags[a + 1, part * HALF:(part + 1) * HALF, :] = both[:, 128:]


def by_slot(lags, put):
    block = lax.broadcasted_iota(jnp.int32, (BLK, 128), 1) // BLK
    odd_block = {d: (block // d) % 2 == 1 for d in (4, 2, 1)}

    @pl.loop(0, ROWS // (2 * BLK))
    def _(tile):
        for sub in range(2):
            rows = pl.ds(pl.multiple_of((2 * tile + sub) * BLK, BLK), BLK)
            for ha in range(2):
                arrays = [lags[8 * ha + k, rows, :] for k in range(8)]
                for d in (4, 2, 1):
                    for k in range(8):
                        if k & d == 0:
                            one, two = arrays[k], arrays[k + d]
                            arrays[k] = jnp.where(odd_block[d], pltpu.roll(two, BLK * d, 1), one)
                            arrays[k + d] = jnp.where(odd_block[d], two, pltpu.roll(one, 128 - BLK * d, 1))
                for k in range(8):
                    put(k, rows, slice(ha * 128, (ha + 1) * 128), arrays[k])


def gram_kernel(tile, live_ref, first_ref, table_ref, left_ref, *refs):
    parts = refs[:len(CHUNKS)]
    outs = refs[len(CHUNKS):-2]
    sums, lags = refs[-2:]
    block = pl.program_id(0)
    bins = left_ref.shape[0]
    first = first_ref[...]
    chosen = [jnp.broadcast_to(first == i, (BLK, 128)) for i in range(3)]

    @pl.loop(0, bins // 32)
    def _(group):
        for step in range(32):
            local_bin = group * 32 + step
            f = block * bins + local_bin
            right = jnp.concatenate(
                [p[0, local_bin, part * n:(part + 1) * n, :] for part in range(2) for p, n in zip(parts, CHUNKS)],
                axis=0,
            )
            cross = jnp.dot(left_ref[local_bin], right, preferred_element_type=jnp.float32)
            for part in range(2):
                blocks = [cross[part * LEFT + i * BLK:part * LEFT + (i + 1) * BLK] for i in range(4)]
                own = blocks[3]
                for i in range(3):
                    own = jnp.where(chosen[i], blocks[i], own)
                for a in range(0, BLK, 8):
                    sums[pl.ds(a * PITCH + part * BINS + f, 8, stride=PITCH), :] = own[a:a + 8]

    @pl.when(block == pl.num_programs(0) - 1)
    def _():
        lag_sums(table_ref, sums, lags)
        live = [live_ref[8 * tile + q] == 1 for q in range(8)]

        def put(q, rows, lanes, value):
            value = jnp.where(live[q], value, 0.0)
            for out in outs:
                if q < out.shape[0]:
                    out[q, rows, lanes] = value.astype(out.dtype)
                    return
                q -= out.shape[0]

        by_slot(lags, put)


def gram(tile, live, first, table, left, parts, counts, dtype):
    step = 32
    shapes = [(n, ROWS, 256) for n in counts]
    return pl.pallas_call(
        functools.partial(gram_kernel, tile),
        grid=(BINS // step,),
        out_shape=[jax.ShapeDtypeStruct(s, dtype) for s in shapes],
        in_specs=[
            pl.BlockSpec(memory_space=pltpu.SMEM),
            pl.BlockSpec((1, 128), lambda k: (0, tile)),
            whole(table.shape),
            pl.BlockSpec((step,) + left.shape[1:], lambda k: (k, 0, 0)),
        ]
        + [pl.BlockSpec((1, step) + p.shape[2:], lambda k: (tile, k, 0, 0)) for p in parts],
        out_specs=[whole(s) for s in shapes],
        scratch_shapes=[
            pltpu.VMEM((BLK * PITCH, 128), jnp.float32),
            pltpu.VMEM((BLK, ROWS, 128), jnp.float32),
        ],
        compiler_params=pltpu.CompilerParams(vmem_limit_bytes=48 * MIB),
        cost_estimate=pl.CostEstimate(flops=16_000_000_000, bytes_accessed=20_000_000, transcendentals=0),
        name="gram",
    )(live, first, table, left, *parts)


def final_kernel(near, low, high, out, later, earlier):
    middle = LAGS // 2

    @pl.loop(0, HALF // BLK)
    def _(tile):
        start = pl.multiple_of(tile * BLK, BLK)
        for q in range(4):
            far = (low, high)[q // 2]
            even, odd = (
                near[q, rows, :] + far[q % 2, rows, :].astype(jnp.float32)
                for rows in (pl.ds(start, BLK), pl.ds(HALF + start, BLK))
            )
            for h in range(2):
                lanes = slice(h * 128, (h + 1) * 128)
                rows = pl.ds(q * (HALF + 1) + start, BLK)
                later[h, rows, :] = even[:, lanes] + odd[:, lanes]
                earlier[h, rows, :] = even[:, lanes] - odd[:, lanes]

    def put(u):
        slots = pl.ds(u, 4, stride=HALF + 1)
        for h in range(2):
            lanes = slice(h * 128, (h + 1) * 128)
            out[middle + u, :, lanes] = later[h, slots, :]
            out[middle - u, :, lanes] = earlier[h, slots, :]

    @pl.loop(0, middle // 20)
    def _(group):
        for k in range(20):
            put(group * 20 + k)

    put(middle)


def final(near, low, high):
    vmem = pl.BlockSpec(memory_space=pltpu.VMEM)
    return pl.pallas_call(
        final_kernel,
        out_shape=jax.ShapeDtypeStruct((LAGS, 4, 256), jnp.float32),
        in_specs=[vmem] * 3,
        out_specs=vmem,
        scratch_shapes=[pltpu.VMEM((2, 4 * (HALF + 1), 128), jnp.float32)] * 2,
        cost_estimate=pl.CostEstimate(flops=10_000_000, bytes_accessed=7_000_000, transcendentals=0),
        name="final",
    )(near, low, high)


def moved(block, axis, to):
    size = lax.axis_size(axis)
    return lax.ppermute(block, axis, [(i, to(i) % size) for i in range(size)])


def one_chip(block):
    return moved(block, "chan", lambda i: i - 2)


def swap(block):
    return moved(block, "chan", lambda i: i ^ 1)


def first_half(block, distance):
    return moved(block[:, :BLK], "chan", lambda i: i - distance)


def local(records, pair_blocks, pair_counts):
    segs = records.shape[0]
    table, backward = make_tables(segs * lax.axis_size("tm"))
    owner = lax.axis_index("chan")
    row = lax.axis_index("tm")

    group = np.array([2, 2, 1, 1, 2, 2, 3, 3, 1, 1, 3, 3, 0, 0, 0, 0], np.int32)
    inside = np.array([0, 1, 2, 3, 2, 3, 0, 1, 0, 1, 2, 3, 0, 1, 2, 3], np.int32)
    order = (row + group) % 4 * 4 + inside
    relative = pair_blocks[order] - 2 * owner
    first = jnp.clip(relative[:, 0], 0, 3)
    right = jnp.clip(relative[:, 1], 0, 10)
    live = (order < pair_counts[0]).astype(jnp.int32)
    odd = (owner % 2).astype(jnp.int32)[None]
    first_lanes = jnp.repeat(first, BLK)[None, :]

    barrier = lax.optimization_barrier
    step = CHUNKS[0]
    x_0, later = barrier((records[:step], records))
    x_1 = later[step:]

    def whitened(c, *pieces):
        return whiten_bins(right, odd, table, [records, b0], pieces, c * step)

    a1_0, b0 = one_chip(x_0), swap(records)
    x_1, a1_0 = barrier((x_1, a1_0))
    a1_1 = one_chip(x_1)
    a2_0, b1_0 = one_chip(a1_0), swap(a1_0)
    b2_0, o5_0 = swap(a2_0), first_half(a2_0, 1)
    part_0 = whitened(0, a1_0, b1_0, a2_0, b2_0, o5_0)
    a1_1, part_0 = barrier((a1_1, part_0))
    a2_1, b1_1 = one_chip(a1_1), swap(a1_1)
    left = left_bins(odd, table, records, b0, [b1_0, b1_1])
    a2_1, left = barrier((a2_1, left))
    b2_1, o5_1 = swap(a2_1), first_half(a2_1, 1)
    part_1 = whitened(1, a1_1, b1_1, a2_1, b2_1, o5_1)

    parts = [part_0, part_1]
    plus, minus = gram(0, live, first_lanes, backward, left, parts, (4, 4), jnp.bfloat16)
    keep, other, own = gram(1, live, first_lanes, backward, left, parts, (2, 2, 4), jnp.float32)

    from_below = moved(plus, "tm", lambda i: i + 1)
    from_above = moved(minus, "tm", lambda i: i - 1)
    up = (keep + from_below[:2].astype(jnp.float32)).astype(jnp.bfloat16)
    down = (other + from_above[:2].astype(jnp.float32)).astype(jnp.bfloat16)
    two_below = moved(up, "tm", lambda i: i + 1)
    two_above = moved(down, "tm", lambda i: i - 1)
    near = own + jnp.concatenate([from_above[2:], from_below[2:]], axis=0).astype(jnp.float32)
    return jnp.transpose(final(near, two_below, two_above), (1, 0, 2))


def solution(mesh):
    return jax.shard_map(
        local,
        mesh=mesh,
        in_specs=(P("tm", "chan", None), P("chan", None), P("chan")),
        out_specs=P(("chan", "tm"), None, None),
        check_vma=False,
    )
```

```python
import functools
import math

import jax
import jax.numpy as jnp
import ml_dtypes
import numpy as np
from jax import lax
from jax.experimental import pallas as pl
from jax.experimental.pallas import tpu as pltpu
from jax.sharding import PartitionSpec as P

LAGS = 401
HALF = 208
ROWS = 2 * HALF
BLK = 16
SLOTS = 16
BINS = 256
LEFT = 64
OWN = 32
BAND = 176
CHUNKS = (32, 32)
PITCH = 513
GROUP = 16

water_share = 0.1
tiny_eps = 1e-06

MIB = 1024 * 1024


def make_tables(segments):
    length = 2 * BINS
    index = np.arange(BINS, dtype=np.int32)
    scale = np.float32(2.0 * math.pi / length)
    radians = (index[:, None] * index[None, :] % length).astype(np.float32) * scale
    forward = np.concatenate([np.cos(radians), -np.sin(radians)], axis=1)
    shift = np.arange(HALF, dtype=np.int32)[:, None]
    lag_radians = (shift * index[None, :] % length).astype(np.float32) * scale
    weight = np.where(index == 0, 1.0, 2.0).astype(np.float32)[None, :] / np.float32(
        math.sqrt(float(BINS * segments))
    )
    waves = np.stack([np.cos(lag_radians) * weight, -np.sin(lag_radians) * weight]).astype(np.float32)
    waves[:, LAGS // 2 + 1:] = 0.0
    high = waves.astype(ml_dtypes.bfloat16)
    low = (waves - high.astype(np.float32)).astype(ml_dtypes.bfloat16)
    return (np.ascontiguousarray(forward.astype(ml_dtypes.bfloat16).T), np.concatenate([high, low], axis=1))


def whiten_tile(spec, lanes, put):
    total = jnp.zeros((8, 128), jnp.float32)
    for f in range(0, BINS, 8):
        real_part = spec[f:f + 8, lanes]
        imag_part = spec[BINS + f:BINS + f + 8, lanes]
        total = total + (real_part * real_part + imag_part * imag_part)
    level = jnp.sum(total, axis=0, keepdims=True) * (1.0 / BINS)
    floor = jnp.broadcast_to(water_share * level + tiny_eps, (8, 128))
    for f in range(0, BINS, 8):
        real_part = spec[f:f + 8, lanes]
        imag_part = spec[BINS + f:BINS + f + 8, lanes]
        inverse = lax.rsqrt(real_part * real_part + imag_part * imag_part + floor)
        put(f, real_part * inverse, imag_part * inverse)


def in_turns(count, transform, whiten, spec_a, spec_b):
    transform(0, spec_a)

    @pl.loop(0, count // 2)
    def _(pair):
        i = 2 * pair
        transform(i + 1, spec_b)
        whiten(i, spec_a)
        transform(jnp.minimum(i + 2, count - 1), spec_a)
        whiten(i + 1, spec_b)


def whiten_kernel(right_ref, odd_ref, table_ref, x0, b0, a1, b1, a2, b2, o5, out_ref,
                  band, spec_a, spec_b, bins_ref, packed, sems):
    segs = a1.shape[0]
    depth = 2 * segs
    pitch = depth + 1
    odd = odd_ref[0] == 1

    @pl.loop(0, segs)
    def _(s):
        band[s, 0:32, :] = x0[s]
        band[s, 32:64, :] = jnp.where(odd, b1[s], b0[s])
        band[s, 64:96, :] = a1[s]
        band[s, 96:128, :] = jnp.where(odd, b2[s], b1[s])
        band[s, 128:160, :] = a2[s]
        band[s, 160:176, :] = o5[s]

    starts = [pl.multiple_of(right_ref[q] * BLK, BLK) for q in range(SLOTS)]

    def transform(s, spec):
        rows = [band[s, pl.ds(start, BLK), :] for start in starts]
        spec[...] = lax.dot_general(
            table_ref[...],
            jnp.concatenate(rows, axis=0),
            (((1,), (1,)), ((), ())),
            preferred_element_type=jnp.float32,
        )

    def whiten(s, spec):
        for h in range(2):
            def put(f, real_part, imag_part):
                bins_ref[h, pl.ds(f * pitch + s, 8, stride=pitch), :] = real_part
                bins_ref[h, pl.ds(f * pitch + segs + s, 8, stride=pitch), :] = imag_part

            whiten_tile(spec, slice(h * 128, (h + 1) * 128), put)

    in_turns(segs, transform, whiten, spec_a, spec_b)

    def copy(group):
        some = pl.ds(group * GROUP, GROUP)
        return pltpu.make_async_copy(packed.at[:, some], out_ref.at[:, some], sems.at[group])

    @pl.loop(0, BINS // GROUP)
    def _(group):
        for step in range(GROUP):
            f = group * GROUP + step
            for h in range(2):
                packed[h, f] = bins_ref[h, pl.ds(f * pitch, depth), :].astype(jnp.bfloat16)
        copy(group).start()

    @pl.loop(0, BINS // GROUP)
    def _(group):
        copy(group).wait()


def whole(shape):
    return pl.BlockSpec(shape, lambda *_: (0,) * len(shape))


def whiten_bins(right, odd, table, whole_pieces, pieces, chunk):
    smem = pl.BlockSpec(memory_space=pltpu.SMEM)
    segs = pieces[0].shape[0]
    share = pl.BlockSpec((segs, 32, BINS), lambda _: (chunk, 0, 0))
    shape = (2, BINS, 2 * segs, 128)
    return pl.pallas_call(
        whiten_kernel,
        grid=(1,),
        out_shape=jax.ShapeDtypeStruct(shape, jnp.bfloat16),
        in_specs=[smem, smem, whole(table.shape), share, share] + [whole(p.shape) for p in pieces],
        out_specs=pl.BlockSpec(memory_space=pl.ANY),
        scratch_shapes=[
            pltpu.VMEM((segs, BAND, BINS), jnp.bfloat16),
            pltpu.VMEM((512, 256), jnp.float32),
            pltpu.VMEM((512, 256), jnp.float32),
            pltpu.VMEM((2, BINS * (2 * segs + 1), 128), jnp.float32),
            pltpu.VMEM(shape, jnp.bfloat16),
            pltpu.SemaphoreType.DMA((BINS // GROUP,)),
        ],
        compiler_params=pltpu.CompilerParams(vmem_limit_bytes=52 * MIB),
        cost_estimate=pl.CostEstimate(flops=240_000_000 * segs, bytes_accessed=8_000_000, transcendentals=0),
        name="whiten",
    )(right, odd, table, *whole_pieces, *pieces)


def left_kernel(odd_ref, table_ref, *refs):
    out_ref, records, spec_a, spec_b, bins_ref, packed, sems = refs[-7:]
    pieces = refs[:-7]
    odd = odd_ref[0] == 1
    segs = pieces[0].shape[0]
    spread = OWN + 1
    pitch = 2 * OWN + 1

    def fill(s, channels):
        channels = channels.astype(jnp.float32)
        for h in range(2):
            records[h, pl.ds(s * spread, OWN), :] = channels[:, h * 128:(h + 1) * 128]

    if len(pieces) == 1:
        @pl.loop(0, segs)
        def _(s):
            fill(s, pieces[0][s])
    else:
        offset = 0
        for piece in pieces[1:]:
            @pl.loop(0, piece.shape[0])
            def _(i, piece=piece, offset=offset):
                fill(offset + i, jnp.where(odd, piece[i], pieces[0][offset + i]))

            offset += piece.shape[0]

    def transform(quad, spec):
        rows = [
            jnp.concatenate([records[h, pl.ds(quad * 4 + k, segs, stride=spread), :] for h in range(2)], axis=1)
            for k in range(4)
        ]
        spec[...] = lax.dot_general(
            table_ref[...],
            jnp.concatenate(rows, axis=0).astype(jnp.bfloat16),
            (((1,), (1,)), ((), ())),
            preferred_element_type=jnp.float32,
        )

    in_first = lax.broadcasted_iota(jnp.int32, (8, 128), 1) < LEFT

    def whiten(quad, spec):
        for h in range(2):
            a = quad * 4 + 2 * h

            def put(f, real_part, imag_part):
                real_other = pltpu.roll(real_part, LEFT, 1)
                imag_other = pltpu.roll(imag_part, LEFT, 1)
                rows = [
                    (a, jnp.where(in_first, real_part, imag_other)),
                    (OWN + a, jnp.where(in_first, imag_part, -real_other)),
                    (a + 1, jnp.where(in_first, real_other, imag_part)),
                    (OWN + a + 1, jnp.where(in_first, imag_other, -real_part)),
                ]
                for row, value in rows:
                    bins_ref[pl.ds(f * pitch + row, 8, stride=pitch), :] = value

            whiten_tile(spec, slice(h * 128, (h + 1) * 128), put)

    in_turns(OWN // 4, transform, whiten, spec_a, spec_b)

    def copy(group):
        some = pl.ds(group * GROUP, GROUP)
        return pltpu.make_async_copy(packed.at[some], out_ref.at[some], sems.at[group])

    @pl.loop(0, BINS // GROUP)
    def _(group):
        for step in range(GROUP):
            f = group * GROUP + step
            packed[f] = bins_ref[pl.ds(f * pitch, 2 * OWN), :].astype(jnp.bfloat16)
        copy(group).start()

    @pl.loop(0, BINS // GROUP)
    def _(group):
        copy(group).wait()


def left_bins(odd, table, pieces):
    vmem = pl.BlockSpec(memory_space=pltpu.VMEM)
    smem = pl.BlockSpec(memory_space=pltpu.SMEM)
    shape = (BINS, 2 * OWN, 128)
    return pl.pallas_call(
        left_kernel,
        out_shape=jax.ShapeDtypeStruct(shape, jnp.bfloat16),
        in_specs=[smem] + [vmem] * (1 + len(pieces)),
        out_specs=pl.BlockSpec(memory_space=pl.ANY),
        scratch_shapes=[
            pltpu.VMEM((2, pieces[0].shape[0] * (OWN + 1), 128), jnp.float32),
            pltpu.VMEM((512, 256), jnp.float32),
            pltpu.VMEM((512, 256), jnp.float32),
            pltpu.VMEM((BINS * (2 * OWN + 1), 128), jnp.float32),
            pltpu.VMEM(shape, jnp.bfloat16),
            pltpu.SemaphoreType.DMA((BINS // GROUP,)),
        ],
        compiler_params=pltpu.CompilerParams(vmem_limit_bytes=48 * MIB),
        cost_estimate=pl.CostEstimate(flops=4_000_000_000, bytes_accessed=8_000_000, transcendentals=0),
        name="left",
    )(odd, table, *pieces)


def lag_sums(table_ref, cross_ref, lags):
    @pl.loop(0, BLK // 8)
    def _(eight):
        for pair in range(4):
            a = 8 * eight + 2 * pair
            for part in range(2):
                cross = jnp.concatenate(
                    [
                        cross_ref[pl.ds((a + k) * PITCH + part * BINS, BINS), :].astype(jnp.bfloat16)
                        for k in range(2)
                    ],
                    axis=1,
                )
                both = jnp.dot(table_ref[part], cross, preferred_element_type=jnp.float32)
                both = both[:HALF] + both[HALF:]
                lags[a, part * HALF:(part + 1) * HALF, :] = both[:, :128]
                lags[a + 1, part * HALF:(part + 1) * HALF, :] = both[:, 128:]


def by_slot(lags, put):
    block = lax.broadcasted_iota(jnp.int32, (BLK, 128), 1) // BLK
    odd_block = {d: (block // d) % 2 == 1 for d in (4, 2, 1)}

    @pl.loop(0, ROWS // (2 * BLK))
    def _(tile):
        for sub in range(2):
            rows = pl.ds(pl.multiple_of((2 * tile + sub) * BLK, BLK), BLK)
            for ha in range(2):
                arrays = [lags[8 * ha + k, rows, :] for k in range(8)]
                for d in (4, 2, 1):
                    for k in range(8):
                        if k & d == 0:
                            one, two = arrays[k], arrays[k + d]
                            arrays[k] = jnp.where(odd_block[d], pltpu.roll(two, BLK * d, 1), one)
                            arrays[k + d] = jnp.where(odd_block[d], two, pltpu.roll(one, 128 - BLK * d, 1))
                for k in range(8):
                    put(k, rows, slice(ha * 128, (ha + 1) * 128), arrays[k])


def gram_kernel(tile, live_ref, first_ref, table_ref, own_ref, next_ref, *refs):
    parts = refs[:len(CHUNKS)]
    outs = refs[len(CHUNKS):-2]
    sums, lags = refs[-2:]
    block = pl.program_id(0)
    bins = own_ref.shape[0]
    first = first_ref[...]
    chosen = [jnp.broadcast_to(first == i, (BLK, 128)) for i in range(3)]

    @pl.loop(0, bins // 32)
    def _(group):
        for step in range(32):
            local_bin = group * 32 + step
            f = block * bins + local_bin
            right = jnp.concatenate(
                [p[0, local_bin, part * n:(part + 1) * n, :] for part in range(2) for p, n in zip(parts, CHUNKS)],
                axis=0,
            )
            left = jnp.concatenate([own_ref[local_bin], next_ref[local_bin]], axis=0)
            cross = jnp.dot(left, right, preferred_element_type=jnp.float32)
            for part in range(2):
                starts = [i // 2 * LEFT + part * OWN + i % 2 * BLK for i in range(4)]
                blocks = [cross[start:start + BLK] for start in starts]
                own = blocks[3]
                for i in range(3):
                    own = jnp.where(chosen[i], blocks[i], own)
                for a in range(0, BLK, 8):
                    sums[pl.ds(a * PITCH + part * BINS + f, 8, stride=PITCH), :] = own[a:a + 8]

    @pl.when(block == pl.num_programs(0) - 1)
    def _():
        lag_sums(table_ref, sums, lags)
        live = [live_ref[8 * tile + q] == 1 for q in range(8)]

        def put(q, rows, lanes, value):
            value = jnp.where(live[q], value, 0.0)
            for out in outs:
                if q < out.shape[0]:
                    out[q, rows, lanes] = value.astype(out.dtype)
                    return
                q -= out.shape[0]

        by_slot(lags, put)


def gram(tile, live, first, table, left, parts, counts, dtype):
    step = 32
    shapes = [(n, ROWS, 256) for n in counts]
    return pl.pallas_call(
        functools.partial(gram_kernel, tile),
        grid=(BINS // step,),
        out_shape=[jax.ShapeDtypeStruct(s, dtype) for s in shapes],
        in_specs=[
            pl.BlockSpec(memory_space=pltpu.SMEM),
            pl.BlockSpec((1, 128), lambda k: (0, tile)),
            whole(table.shape),
        ]
        + [pl.BlockSpec((step,) + p.shape[1:], lambda k: (k, 0, 0)) for p in left]
        + [pl.BlockSpec((1, step) + p.shape[2:], lambda k: (tile, k, 0, 0)) for p in parts],
        out_specs=[whole(s) for s in shapes],
        scratch_shapes=[
            pltpu.VMEM((BLK * PITCH, 128), jnp.float32),
            pltpu.VMEM((BLK, ROWS, 128), jnp.float32),
        ],
        compiler_params=pltpu.CompilerParams(vmem_limit_bytes=48 * MIB),
        cost_estimate=pl.CostEstimate(flops=16_000_000_000, bytes_accessed=20_000_000, transcendentals=0),
        name="gram",
    )(live, first, table, *left, *parts)


def final_kernel(near, low, high, out, later, earlier):
    middle = LAGS // 2

    @pl.loop(0, HALF // BLK)
    def _(tile):
        start = pl.multiple_of(tile * BLK, BLK)
        for q in range(4):
            far = (low, high)[q // 2]
            even, odd = (
                near[q, rows, :] + far[q % 2, rows, :].astype(jnp.float32)
                for rows in (pl.ds(start, BLK), pl.ds(HALF + start, BLK))
            )
            for h in range(2):
                lanes = slice(h * 128, (h + 1) * 128)
                rows = pl.ds(q * (HALF + 1) + start, BLK)
                later[h, rows, :] = even[:, lanes] + odd[:, lanes]
                earlier[h, rows, :] = even[:, lanes] - odd[:, lanes]

    def put(u):
        slots = pl.ds(u, 4, stride=HALF + 1)
        for h in range(2):
            lanes = slice(h * 128, (h + 1) * 128)
            out[middle + u, :, lanes] = later[h, slots, :]
            out[middle - u, :, lanes] = earlier[h, slots, :]

    @pl.loop(0, middle // 20)
    def _(group):
        for k in range(20):
            put(group * 20 + k)

    put(middle)


def final(near, low, high):
    vmem = pl.BlockSpec(memory_space=pltpu.VMEM)
    return pl.pallas_call(
        final_kernel,
        out_shape=jax.ShapeDtypeStruct((LAGS, 4, 256), jnp.float32),
        in_specs=[vmem] * 3,
        out_specs=vmem,
        scratch_shapes=[pltpu.VMEM((2, 4 * (HALF + 1), 128), jnp.float32)] * 2,
        cost_estimate=pl.CostEstimate(flops=10_000_000, bytes_accessed=7_000_000, transcendentals=0),
        name="final",
    )(near, low, high)


def moved(block, axis, to):
    size = lax.axis_size(axis)
    return lax.ppermute(block, axis, [(i, to(i) % size) for i in range(size)])


def one_chip(block):
    return moved(block, "chan", lambda i: i - 2)


def swap(block):
    return moved(block, "chan", lambda i: i ^ 1)


def first_half(block, distance):
    return moved(block[:, :BLK], "chan", lambda i: i - distance)


def local(records, pair_blocks, pair_counts):
    segs = records.shape[0]
    table, backward = make_tables(segs * lax.axis_size("tm"))
    owner = lax.axis_index("chan")
    row = lax.axis_index("tm")

    group = np.array([2, 2, 1, 1, 2, 2, 3, 3, 1, 1, 3, 3, 0, 0, 0, 0], np.int32)
    inside = np.array([0, 1, 2, 3, 2, 3, 0, 1, 0, 1, 2, 3, 0, 1, 2, 3], np.int32)
    order = (row + group) % 4 * 4 + inside
    relative = pair_blocks[order] - 2 * owner
    first = jnp.clip(relative[:, 0], 0, 3)
    right = jnp.clip(relative[:, 1], 0, 10)
    live = (order < pair_counts[0]).astype(jnp.int32)
    odd = (owner % 2).astype(jnp.int32)[None]
    first_lanes = jnp.repeat(first, BLK)[None, :]

    barrier = lax.optimization_barrier
    step = CHUNKS[0]
    x_0, x_1 = records[:step], records[step:]

    def whitened(c, *pieces):
        return whiten_bins(right, odd, table, [records, b0], pieces, c)

    a1_0, a1_1, b0 = one_chip(x_0), one_chip(x_1), swap(records)
    left_own = left_bins(odd, table, [records])
    a1_0, left_own = barrier((a1_0, left_own))
    a2_0, b1_0 = one_chip(a1_0), swap(a1_0)
    a2_1, b1_1 = one_chip(a1_1), swap(a1_1)
    b2_0, o5_0 = swap(a2_0), first_half(a2_0, 1)
    part_0 = whitened(0, a1_0, b1_0, a2_0, b2_0, o5_0)
    a2_1, b1_1, part_0 = barrier((a2_1, b1_1, part_0))
    b2_1, o5_1 = swap(a2_1), first_half(a2_1, 1)
    left_next = left_bins(odd, table, [b0, b1_0, b1_1])
    part_1 = whitened(1, a1_1, b1_1, a2_1, b2_1, o5_1)

    left = [left_own, left_next]
    parts = [part_0, part_1]
    plus, minus = gram(0, live, first_lanes, backward, left, parts, (4, 4), jnp.bfloat16)
    keep, other, own = gram(1, live, first_lanes, backward, left, parts, (2, 2, 4), jnp.float32)

    from_below = moved(plus, "tm", lambda i: i + 1)
    from_above = moved(minus, "tm", lambda i: i - 1)
    up = (keep + from_below[:2].astype(jnp.float32)).astype(jnp.bfloat16)
    down = (other + from_above[:2].astype(jnp.float32)).astype(jnp.bfloat16)
    two_below = moved(up, "tm", lambda i: i + 1)
    two_above = moved(down, "tm", lambda i: i - 1)
    near = own + jnp.concatenate([from_above[2:], from_below[2:]], axis=0).astype(jnp.float32)
    return jnp.transpose(final(near, two_below, two_above), (1, 0, 2))


def solution(mesh):
    return jax.shard_map(
        local,
        mesh=mesh,
        in_specs=(P("tm", "chan", None), P("chan", None), P("chan")),
        out_specs=P(("chan", "tm"), None, None),
        check_vma=False,
    )
```

```python
import functools
import math

import jax
import jax.numpy as jnp
import ml_dtypes
import numpy as np
from jax import lax
from jax.experimental import pallas as pl
from jax.experimental.pallas import tpu as pltpu
from jax.sharding import PartitionSpec as P

LAGS = 401
HALF = 208
ROWS = 2 * HALF
BLK = 16
SLOTS = 16
BINS = 256
LEFT = 64
OWN = 32
BAND = 176
CHUNKS = (32, 32)
PITCH = 513
GROUP = 16

water_share = 0.1
tiny_eps = 1e-06

MIB = 1024 * 1024


def make_tables(segments):
    length = 2 * BINS
    index = np.arange(BINS, dtype=np.int32)
    scale = np.float32(2.0 * math.pi / length)
    radians = (index[:, None] * index[None, :] % length).astype(np.float32) * scale
    forward = np.concatenate([np.cos(radians), -np.sin(radians)], axis=1)
    shift = np.arange(HALF, dtype=np.int32)[:, None]
    lag_radians = (shift * index[None, :] % length).astype(np.float32) * scale
    weight = np.where(index == 0, 1.0, 2.0).astype(np.float32)[None, :] / np.float32(
        math.sqrt(float(BINS * segments))
    )
    waves = np.stack([np.cos(lag_radians) * weight, -np.sin(lag_radians) * weight]).astype(np.float32)
    waves[:, LAGS // 2 + 1:] = 0.0
    high = waves.astype(ml_dtypes.bfloat16)
    low = (waves - high.astype(np.float32)).astype(ml_dtypes.bfloat16)
    return (np.ascontiguousarray(forward.astype(ml_dtypes.bfloat16).T), np.concatenate([high, low], axis=1))


def whiten_tile(spec, lanes, put):
    total = jnp.zeros((8, 128), jnp.float32)
    for f in range(0, BINS, 8):
        real_part = spec[f:f + 8, lanes]
        imag_part = spec[BINS + f:BINS + f + 8, lanes]
        total = total + (real_part * real_part + imag_part * imag_part)
    level = jnp.sum(total, axis=0, keepdims=True) * (1.0 / BINS)
    floor = jnp.broadcast_to(water_share * level + tiny_eps, (8, 128))
    for f in range(0, BINS, 8):
        real_part = spec[f:f + 8, lanes]
        imag_part = spec[BINS + f:BINS + f + 8, lanes]
        inverse = lax.rsqrt(real_part * real_part + imag_part * imag_part + floor)
        put(f, real_part * inverse, imag_part * inverse)


def in_turns(count, transform, whiten, spec_a, spec_b):
    transform(0, spec_a)

    @pl.loop(0, count // 2)
    def _(pair):
        i = 2 * pair
        transform(i + 1, spec_b)
        whiten(i, spec_a)
        transform(jnp.minimum(i + 2, count - 1), spec_a)
        whiten(i + 1, spec_b)


def whiten_kernel(chunk, right_ref, odd_ref, table_ref, x0, b0, a1, b1, a2, b2, o5, out_ref,
                  band, spec_a, spec_b, bins_ref, packed, sems, band_sems):
    segs = a1.shape[0]
    depth = 2 * segs
    pitch = depth + 1
    odd = odd_ref[0] == 1
    share = pl.ds(chunk * segs, segs)

    def fetch(source, place, channels=32):
        return pltpu.make_async_copy(source, band.at[:, pl.ds(32 * place, channels)], band_sems.at[place])

    fetch(x0.at[share], 0).start()
    fetch(a1, 2).start()
    fetch(a2, 4).start()

    @pl.when(odd)
    def _():
        fetch(b1, 1).start()
        fetch(b2, 3).start()
        fetch(o5, 5, BLK).start()

    @pl.when(jnp.logical_not(odd))
    def _():
        fetch(b0.at[share], 1).start()
        fetch(b1, 3).start()
        fetch(b2.at[:, pl.ds(0, BLK)], 5, BLK).start()

    for place in range(5):
        fetch(a1, place).wait()
    fetch(o5, 5, BLK).wait()

    starts = [pl.multiple_of(right_ref[q] * BLK, BLK) for q in range(SLOTS)]

    def transform(s, spec):
        rows = [band[s, pl.ds(start, BLK), :] for start in starts]
        spec[...] = lax.dot_general(
            table_ref[...],
            jnp.concatenate(rows, axis=0),
            (((1,), (1,)), ((), ())),
            preferred_element_type=jnp.float32,
        )

    def whiten(s, spec):
        for h in range(2):
            def put(f, real_part, imag_part):
                bins_ref[h, pl.ds(f * pitch + s, 8, stride=pitch), :] = real_part
                bins_ref[h, pl.ds(f * pitch + segs + s, 8, stride=pitch), :] = imag_part

            whiten_tile(spec, slice(h * 128, (h + 1) * 128), put)

    in_turns(segs, transform, whiten, spec_a, spec_b)

    def copy(group):
        some = pl.ds(group * GROUP, GROUP)
        return pltpu.make_async_copy(packed.at[:, some], out_ref.at[:, some], sems.at[group])

    @pl.loop(0, BINS // GROUP)
    def _(group):
        for step in range(GROUP):
            f = group * GROUP + step
            for h in range(2):
                packed[h, f] = bins_ref[h, pl.ds(f * pitch, depth), :].astype(jnp.bfloat16)
        copy(group).start()

    @pl.loop(0, BINS // GROUP)
    def _(group):
        copy(group).wait()


def whole(shape):
    return pl.BlockSpec(shape, lambda *_: (0,) * len(shape))


def whiten_bins(right, odd, table, whole_pieces, pieces, chunk):
    smem = pl.BlockSpec(memory_space=pltpu.SMEM)
    anywhere = pl.BlockSpec(memory_space=pl.ANY)
    segs = pieces[0].shape[0]
    shape = (2, BINS, 2 * segs, 128)
    return pl.pallas_call(
        functools.partial(whiten_kernel, chunk),
        out_shape=jax.ShapeDtypeStruct(shape, jnp.bfloat16),
        in_specs=[smem, smem, pl.BlockSpec(memory_space=pltpu.VMEM)] + [anywhere] * (2 + len(pieces)),
        out_specs=pl.BlockSpec(memory_space=pl.ANY),
        scratch_shapes=[
            pltpu.VMEM((segs, BAND, BINS), jnp.bfloat16),
            pltpu.VMEM((512, 256), jnp.float32),
            pltpu.VMEM((512, 256), jnp.float32),
            pltpu.VMEM((2, BINS * (2 * segs + 1), 128), jnp.float32),
            pltpu.VMEM(shape, jnp.bfloat16),
            pltpu.SemaphoreType.DMA((BINS // GROUP,)),
            pltpu.SemaphoreType.DMA((6,)),
        ],
        compiler_params=pltpu.CompilerParams(vmem_limit_bytes=52 * MIB),
        cost_estimate=pl.CostEstimate(flops=240_000_000 * segs, bytes_accessed=8_000_000, transcendentals=0),
        name="whiten",
    )(right, odd, table, *whole_pieces, *pieces)


def left_kernel(odd_ref, table_ref, *refs):
    out_ref, records, spec_a, spec_b, bins_ref, packed, sems = refs[-7:]
    pieces = refs[:-7]
    odd = odd_ref[0] == 1
    segs = pieces[0].shape[0]
    spread = OWN + 1
    pitch = 2 * OWN + 1

    def fill(s, channels):
        channels = channels.astype(jnp.float32)
        for h in range(2):
            records[h, pl.ds(s * spread, OWN), :] = channels[:, h * 128:(h + 1) * 128]

    if len(pieces) == 1:
        @pl.loop(0, segs)
        def _(s):
            fill(s, pieces[0][s])
    else:
        offset = 0
        for piece in pieces[1:]:
            @pl.loop(0, piece.shape[0])
            def _(i, piece=piece, offset=offset):
                fill(offset + i, jnp.where(odd, piece[i], pieces[0][offset + i]))

            offset += piece.shape[0]

    def transform(quad, spec):
        rows = [
            jnp.concatenate([records[h, pl.ds(quad * 4 + k, segs, stride=spread), :] for h in range(2)], axis=1)
            for k in range(4)
        ]
        spec[...] = lax.dot_general(
            table_ref[...],
            jnp.concatenate(rows, axis=0).astype(jnp.bfloat16),
            (((1,), (1,)), ((), ())),
            preferred_element_type=jnp.float32,
        )

    in_first = lax.broadcasted_iota(jnp.int32, (8, 128), 1) < LEFT

    def whiten(quad, spec):
        for h in range(2):
            a = quad * 4 + 2 * h

            def put(f, real_part, imag_part):
                real_other = pltpu.roll(real_part, LEFT, 1)
                imag_other = pltpu.roll(imag_part, LEFT, 1)
                rows = [
                    (a, jnp.where(in_first, real_part, imag_other)),
                    (OWN + a, jnp.where(in_first, imag_part, -real_other)),
                    (a + 1, jnp.where(in_first, real_other, imag_part)),
                    (OWN + a + 1, jnp.where(in_first, imag_other, -real_part)),
                ]
                for row, value in rows:
                    bins_ref[pl.ds(f * pitch + row, 8, stride=pitch), :] = value

            whiten_tile(spec, slice(h * 128, (h + 1) * 128), put)

    in_turns(OWN // 4, transform, whiten, spec_a, spec_b)

    def copy(group):
        some = pl.ds(group * GROUP, GROUP)
        return pltpu.make_async_copy(packed.at[some], out_ref.at[some], sems.at[group])

    @pl.loop(0, BINS // GROUP)
    def _(group):
        for step in range(GROUP):
            f = group * GROUP + step
            packed[f] = bins_ref[pl.ds(f * pitch, 2 * OWN), :].astype(jnp.bfloat16)
        copy(group).start()

    @pl.loop(0, BINS // GROUP)
    def _(group):
        copy(group).wait()


def left_bins(odd, table, pieces):
    vmem = pl.BlockSpec(memory_space=pltpu.VMEM)
    smem = pl.BlockSpec(memory_space=pltpu.SMEM)
    shape = (BINS, 2 * OWN, 128)
    return pl.pallas_call(
        left_kernel,
        out_shape=jax.ShapeDtypeStruct(shape, jnp.bfloat16),
        in_specs=[smem] + [vmem] * (1 + len(pieces)),
        out_specs=pl.BlockSpec(memory_space=pl.ANY),
        scratch_shapes=[
            pltpu.VMEM((2, pieces[0].shape[0] * (OWN + 1), 128), jnp.float32),
            pltpu.VMEM((512, 256), jnp.float32),
            pltpu.VMEM((512, 256), jnp.float32),
            pltpu.VMEM((BINS * (2 * OWN + 1), 128), jnp.float32),
            pltpu.VMEM(shape, jnp.bfloat16),
            pltpu.SemaphoreType.DMA((BINS // GROUP,)),
        ],
        compiler_params=pltpu.CompilerParams(vmem_limit_bytes=48 * MIB),
        cost_estimate=pl.CostEstimate(flops=4_000_000_000, bytes_accessed=8_000_000, transcendentals=0),
        name="left",
    )(odd, table, *pieces)


def lag_sums(table_ref, cross_ref, lags):
    @pl.loop(0, BLK // 8)
    def _(eight):
        for pair in range(4):
            a = 8 * eight + 2 * pair
            for part in range(2):
                cross = jnp.concatenate(
                    [
                        cross_ref[pl.ds((a + k) * PITCH + part * BINS, BINS), :].astype(jnp.bfloat16)
                        for k in range(2)
                    ],
                    axis=1,
                )
                both = jnp.dot(table_ref[part], cross, preferred_element_type=jnp.float32)
                both = both[:HALF] + both[HALF:]
                lags[a, part * HALF:(part + 1) * HALF, :] = both[:, :128]
                lags[a + 1, part * HALF:(part + 1) * HALF, :] = both[:, 128:]


def by_slot(lags, put):
    block = lax.broadcasted_iota(jnp.int32, (BLK, 128), 1) // BLK
    odd_block = {d: (block // d) % 2 == 1 for d in (4, 2, 1)}

    @pl.loop(0, ROWS // (2 * BLK))
    def _(tile):
        for sub in range(2):
            rows = pl.ds(pl.multiple_of((2 * tile + sub) * BLK, BLK), BLK)
            for ha in range(2):
                arrays = [lags[8 * ha + k, rows, :] for k in range(8)]
                for d in (4, 2, 1):
                    for k in range(8):
                        if k & d == 0:
                            one, two = arrays[k], arrays[k + d]
                            arrays[k] = jnp.where(odd_block[d], pltpu.roll(two, BLK * d, 1), one)
                            arrays[k + d] = jnp.where(odd_block[d], two, pltpu.roll(one, 128 - BLK * d, 1))
                for k in range(8):
                    put(k, rows, slice(ha * 128, (ha + 1) * 128), arrays[k])


def gram_kernel(tile, live_ref, first_ref, table_ref, own_ref, next_ref, *refs):
    parts = refs[:len(CHUNKS)]
    outs = refs[len(CHUNKS):-2]
    sums, lags = refs[-2:]
    block = pl.program_id(0)
    bins = own_ref.shape[0]
    first = first_ref[...]
    chosen = [jnp.broadcast_to(first == i, (BLK, 128)) for i in range(3)]

    @pl.loop(0, bins // 32)
    def _(group):
        for step in range(32):
            local_bin = group * 32 + step
            f = block * bins + local_bin
            right = jnp.concatenate(
                [p[0, local_bin, part * n:(part + 1) * n, :] for part in range(2) for p, n in zip(parts, CHUNKS)],
                axis=0,
            )
            left = jnp.concatenate([own_ref[local_bin], next_ref[local_bin]], axis=0)
            cross = jnp.dot(left, right, preferred_element_type=jnp.float32)
            for part in range(2):
                starts = [i // 2 * LEFT + part * OWN + i % 2 * BLK for i in range(4)]
                blocks = [cross[start:start + BLK] for start in starts]
                own = blocks[3]
                for i in range(3):
                    own = jnp.where(chosen[i], blocks[i], own)
                for a in range(0, BLK, 8):
                    sums[pl.ds(a * PITCH + part * BINS + f, 8, stride=PITCH), :] = own[a:a + 8]

    @pl.when(block == pl.num_programs(0) - 1)
    def _():
        lag_sums(table_ref, sums, lags)
        live = [live_ref[8 * tile + q] == 1 for q in range(8)]

        def put(q, rows, lanes, value):
            value = jnp.where(live[q], value, 0.0)
            for out in outs:
                if q < out.shape[0]:
                    out[q, rows, lanes] = value.astype(out.dtype)
                    return
                q -= out.shape[0]

        by_slot(lags, put)


def gram(tile, live, first, table, left, parts, counts, dtype):
    step = 32
    shapes = [(n, ROWS, 256) for n in counts]
    return pl.pallas_call(
        functools.partial(gram_kernel, tile),
        grid=(BINS // step,),
        out_shape=[jax.ShapeDtypeStruct(s, dtype) for s in shapes],
        in_specs=[
            pl.BlockSpec(memory_space=pltpu.SMEM),
            pl.BlockSpec((1, 128), lambda k: (0, tile)),
            whole(table.shape),
        ]
        + [pl.BlockSpec((step,) + p.shape[1:], lambda k: (k, 0, 0)) for p in left]
        + [pl.BlockSpec((1, step) + p.shape[2:], lambda k: (tile, k, 0, 0)) for p in parts],
        out_specs=[whole(s) for s in shapes],
        scratch_shapes=[
            pltpu.VMEM((BLK * PITCH, 128), jnp.float32),
            pltpu.VMEM((BLK, ROWS, 128), jnp.float32),
        ],
        compiler_params=pltpu.CompilerParams(vmem_limit_bytes=48 * MIB),
        cost_estimate=pl.CostEstimate(flops=16_000_000_000, bytes_accessed=20_000_000, transcendentals=0),
        name="gram",
    )(live, first, table, *left, *parts)


def final_kernel(near_any, low_any, high_any, out, near, low, high, later, earlier, sems):
    middle = LAGS // 2
    copies = [
        pltpu.make_async_copy(source, target, sems.at[k])
        for k, (source, target) in enumerate(((near_any, near), (low_any, low), (high_any, high)))
    ]
    for copy in copies:
        copy.start()
    for copy in copies:
        copy.wait()

    @pl.loop(0, HALF // BLK)
    def _(tile):
        start = pl.multiple_of(tile * BLK, BLK)
        for q in range(4):
            far = (low, high)[q // 2]
            even, odd = (
                near[q, rows, :] + far[q % 2, rows, :].astype(jnp.float32)
                for rows in (pl.ds(start, BLK), pl.ds(HALF + start, BLK))
            )
            for h in range(2):
                lanes = slice(h * 128, (h + 1) * 128)
                rows = pl.ds(q * (HALF + 1) + start, BLK)
                later[h, rows, :] = even[:, lanes] + odd[:, lanes]
                earlier[h, rows, :] = even[:, lanes] - odd[:, lanes]

    def put(u):
        slots = pl.ds(u, 4, stride=HALF + 1)
        for h in range(2):
            lanes = slice(h * 128, (h + 1) * 128)
            out[middle + u, :, lanes] = later[h, slots, :]
            out[middle - u, :, lanes] = earlier[h, slots, :]

    @pl.loop(0, middle // 20)
    def _(group):
        for k in range(20):
            put(group * 20 + k)

    put(middle)


def final(near, low, high):
    vmem = pl.BlockSpec(memory_space=pltpu.VMEM)
    return pl.pallas_call(
        final_kernel,
        out_shape=jax.ShapeDtypeStruct((LAGS, 4, 256), jnp.float32),
        in_specs=[pl.BlockSpec(memory_space=pl.ANY)] * 3,
        out_specs=vmem,
        scratch_shapes=[pltpu.VMEM(x.shape, x.dtype) for x in (near, low, high)]
        + [pltpu.VMEM((2, 4 * (HALF + 1), 128), jnp.float32)] * 2
        + [pltpu.SemaphoreType.DMA((3,))],
        cost_estimate=pl.CostEstimate(flops=10_000_000, bytes_accessed=7_000_000, transcendentals=0),
        name="final",
    )(near, low, high)


def moved(block, axis, to):
    size = lax.axis_size(axis)
    return lax.ppermute(block, axis, [(i, to(i) % size) for i in range(size)])


def one_chip(block):
    return moved(block, "chan", lambda i: i - 2)


def swap(block):
    return moved(block, "chan", lambda i: i ^ 1)


def first_half(block):
    return moved(block[:, :BLK], "chan", lambda i: i - 1)


def one_row(block, step):
    return moved(block, "tm", lambda i: i + step)


def local(records, pair_blocks, pair_counts):
    segs = records.shape[0]
    table, backward = make_tables(segs * lax.axis_size("tm"))
    owner = lax.axis_index("chan")
    row = lax.axis_index("tm")

    group = np.array([2, 2, 1, 1, 2, 2, 3, 3, 1, 1, 3, 3, 0, 0, 0, 0], np.int32)
    inside = np.array([0, 1, 2, 3, 2, 3, 0, 1, 0, 1, 2, 3, 0, 1, 2, 3], np.int32)
    order = (row + group) % 4 * 4 + inside
    relative = pair_blocks[order] - 2 * owner
    first = jnp.clip(relative[:, 0], 0, 3)
    right = jnp.clip(relative[:, 1], 0, 10)
    live = (order < pair_counts[0]).astype(jnp.int32)
    odd = (owner % 2).astype(jnp.int32)[None]
    first_lanes = jnp.repeat(first, BLK)[None, :]

    barrier = lax.optimization_barrier
    step = CHUNKS[0]
    x_0, later = barrier((records[:step], records))
    x_1 = later[step:]

    def whitened(c, *pieces):
        return whiten_bins(right, odd, table, [records, b0], pieces, c)

    a1_0, a1_1, b0 = one_chip(x_0), one_chip(x_1), swap(records)
    left_own = left_bins(odd, table, [records])
    a1_0, left_own = barrier((a1_0, left_own))
    a2_0, b1_0 = one_chip(a1_0), swap(a1_0)
    a2_1, b1_1 = one_chip(a1_1), swap(a1_1)
    b2_0, o5_0 = swap(a2_0), first_half(a2_0)
    part_0 = whitened(0, a1_0, b1_0, a2_0, b2_0, o5_0)
    a2_1, b1_1, part_0 = barrier((a2_1, b1_1, part_0))
    b2_1, o5_1 = swap(a2_1), first_half(a2_1)
    left_next = left_bins(odd, table, [b0, b1_0, b1_1])
    part_1 = whitened(1, a1_1, b1_1, a2_1, b2_1, o5_1)

    left = [left_own, left_next]
    parts = [part_0, part_1]
    relay_up, plain_up, relay_down, plain_down = gram(
        0, live, first_lanes, backward, left, parts, (2, 2, 2, 2), jnp.bfloat16
    )
    up_in, down_in = one_row(relay_up, 1), one_row(relay_down, -1)
    plain_below, plain_above = one_row(plain_up, 1), one_row(plain_down, -1)
    keep, other, own = gram(1, live, first_lanes, backward, left, parts, (2, 2, 4), jnp.float32)

    f32 = jnp.float32
    two_below = one_row((keep + up_in.astype(f32)).astype(jnp.bfloat16), 1)
    two_above = one_row((other + down_in.astype(f32)).astype(jnp.bfloat16), -1)
    near = own + jnp.concatenate([plain_above, plain_below], axis=0).astype(f32)
    return jnp.transpose(final(near, two_below, two_above), (1, 0, 2))


def solution(mesh):
    return jax.shard_map(
        local,
        mesh=mesh,
        in_specs=(P("tm", "chan", None), P("chan", None), P("chan")),
        out_specs=P(("chan", "tm"), None, None),
        check_vma=False,
    )
```

```python
import functools
import math

import jax
import jax.numpy as jnp
import ml_dtypes
import numpy as np
from jax import lax
from jax.experimental import pallas as pl
from jax.experimental.pallas import tpu as pltpu
from jax.sharding import PartitionSpec as P

LAGS = 401
HALF = 208
ROWS = 2 * HALF
BLK = 16
SLOTS = 16
BINS = 256
LEFT = 64
OWN = 32
BAND = 176
CHUNKS = (32, 32)
PITCH = 513
GROUP = 16
BLOCK = 32

water_share = 0.1
tiny_eps = 1e-06

MIB = 1024 * 1024


def make_tables(segments):
    length = 2 * BINS
    index = np.arange(BINS, dtype=np.int32)
    scale = np.float32(2.0 * math.pi / length)
    radians = (index[:, None] * index[None, :] % length).astype(np.float32) * scale
    forward = np.concatenate([np.cos(radians), -np.sin(radians)], axis=1)
    shift = np.arange(HALF, dtype=np.int32)[:, None]
    lag_radians = (shift * index[None, :] % length).astype(np.float32) * scale
    weight = np.where(index == 0, 1.0, 2.0).astype(np.float32)[None, :] / np.float32(
        math.sqrt(float(BINS * segments))
    )
    waves = np.stack([np.cos(lag_radians) * weight, -np.sin(lag_radians) * weight]).astype(np.float32)
    waves[:, LAGS // 2 + 1:] = 0.0
    high = waves.astype(ml_dtypes.bfloat16)
    low = (waves - high.astype(np.float32)).astype(ml_dtypes.bfloat16)
    return (np.ascontiguousarray(forward.astype(ml_dtypes.bfloat16).T), np.concatenate([high, low], axis=1))


def whiten_tile(spec, lanes, put):
    total = jnp.zeros((8, 128), jnp.float32)
    for f in range(0, BINS, 8):
        real_part = spec[f:f + 8, lanes]
        imag_part = spec[BINS + f:BINS + f + 8, lanes]
        total = total + (real_part * real_part + imag_part * imag_part)
    level = jnp.sum(total, axis=0, keepdims=True) * (1.0 / BINS)
    floor = jnp.broadcast_to(water_share * level + tiny_eps, (8, 128))
    for f in range(0, BINS, 8):
        real_part = spec[f:f + 8, lanes]
        imag_part = spec[BINS + f:BINS + f + 8, lanes]
        inverse = lax.rsqrt(real_part * real_part + imag_part * imag_part + floor)
        put(f, real_part * inverse, imag_part * inverse)


def in_turns(count, transform, whiten, spec_a, spec_b):
    transform(0, spec_a)

    @pl.loop(0, count // 2)
    def _(pair):
        i = 2 * pair
        transform(i + 1, spec_b)
        whiten(i, spec_a)
        transform(jnp.minimum(i + 2, count - 1), spec_a)
        whiten(i + 1, spec_b)


def whiten_kernel(chunk, right_ref, odd_ref, table_ref, x0, b0, a1, b1, a2, b2, o5, out_ref,
                  band, spec_a, spec_b, bins_ref, packed, sems, band_sems):
    segs = a1.shape[0]
    depth = 2 * segs
    pitch = depth + 1
    odd = odd_ref[0] == 1
    share = pl.ds(chunk * segs, segs)

    def fetch(source, place, channels=32):
        return pltpu.make_async_copy(source, band.at[:, pl.ds(32 * place, channels)], band_sems.at[place])

    fetch(x0.at[share], 0).start()
    fetch(a1, 2).start()
    fetch(a2, 4).start()

    @pl.when(odd)
    def _():
        fetch(b1, 1).start()
        fetch(b2, 3).start()
        fetch(o5, 5, BLK).start()

    @pl.when(jnp.logical_not(odd))
    def _():
        fetch(b0.at[share], 1).start()
        fetch(b1, 3).start()
        fetch(b2.at[:, pl.ds(0, BLK)], 5, BLK).start()

    for place in range(5):
        fetch(a1, place).wait()
    fetch(o5, 5, BLK).wait()

    starts = [pl.multiple_of(right_ref[q] * BLK, BLK) for q in range(SLOTS)]

    def transform(s, spec):
        rows = [band[s, pl.ds(start, BLK), :] for start in starts]
        spec[...] = lax.dot_general(
            table_ref[...],
            jnp.concatenate(rows, axis=0),
            (((1,), (1,)), ((), ())),
            preferred_element_type=jnp.float32,
        )

    def whiten(s, spec):
        for h in range(2):
            def put(f, real_part, imag_part):
                bins_ref[h, pl.ds(f * pitch + s, 8, stride=pitch), :] = real_part
                bins_ref[h, pl.ds(f * pitch + segs + s, 8, stride=pitch), :] = imag_part

            whiten_tile(spec, slice(h * 128, (h + 1) * 128), put)

    in_turns(segs, transform, whiten, spec_a, spec_b)

    def copy(group):
        some = pl.ds(group * GROUP, GROUP)
        return pltpu.make_async_copy(packed.at[:, some], out_ref.at[:, some], sems.at[group])

    @pl.loop(0, BINS // GROUP)
    def _(group):
        for step in range(GROUP):
            f = group * GROUP + step
            for h in range(2):
                packed[h, f] = bins_ref[h, pl.ds(f * pitch, depth), :].astype(jnp.bfloat16)
        copy(group).start()

    @pl.loop(0, BINS // GROUP)
    def _(group):
        copy(group).wait()


def whole(shape):
    return pl.BlockSpec(shape, lambda *_: (0,) * len(shape))


def whiten_bins(right, odd, table, whole_pieces, pieces, chunk):
    smem = pl.BlockSpec(memory_space=pltpu.SMEM)
    anywhere = pl.BlockSpec(memory_space=pl.ANY)
    segs = pieces[0].shape[0]
    shape = (2, BINS, 2 * segs, 128)
    return pl.pallas_call(
        functools.partial(whiten_kernel, chunk),
        out_shape=jax.ShapeDtypeStruct(shape, jnp.bfloat16),
        in_specs=[smem, smem, pl.BlockSpec(memory_space=pltpu.VMEM)] + [anywhere] * (2 + len(pieces)),
        out_specs=pl.BlockSpec(memory_space=pl.ANY),
        scratch_shapes=[
            pltpu.VMEM((segs, BAND, BINS), jnp.bfloat16),
            pltpu.VMEM((512, 256), jnp.float32),
            pltpu.VMEM((512, 256), jnp.float32),
            pltpu.VMEM((2, BINS * (2 * segs + 1), 128), jnp.float32),
            pltpu.VMEM(shape, jnp.bfloat16),
            pltpu.SemaphoreType.DMA((BINS // GROUP,)),
            pltpu.SemaphoreType.DMA((6,)),
        ],
        compiler_params=pltpu.CompilerParams(vmem_limit_bytes=52 * MIB),
        cost_estimate=pl.CostEstimate(flops=240_000_000 * segs, bytes_accessed=8_000_000, transcendentals=0),
        name="whiten",
    )(right, odd, table, *whole_pieces, *pieces)


def left_kernel(odd_ref, table_ref, *refs):
    count = (len(refs) - 8) // 2
    sources, pieces = refs[:count], refs[-count:]
    out_ref, records, spec_a, spec_b, bins_ref, packed, sems, piece_sems = refs[count:-count]
    fetches = [
        pltpu.make_async_copy(source, piece, piece_sems.at[k])
        for k, (source, piece) in enumerate(zip(sources, pieces))
    ]
    for fetch in fetches:
        fetch.start()
    for fetch in fetches:
        fetch.wait()
    odd = odd_ref[0] == 1
    segs = pieces[0].shape[0]
    spread = OWN + 1
    pitch = 2 * OWN + 1

    def fill(s, channels):
        channels = channels.astype(jnp.float32)
        for h in range(2):
            records[h, pl.ds(s * spread, OWN), :] = channels[:, h * 128:(h + 1) * 128]

    if len(pieces) == 1:
        @pl.loop(0, segs)
        def _(s):
            fill(s, pieces[0][s])
    else:
        offset = 0
        for piece in pieces[1:]:
            @pl.loop(0, piece.shape[0])
            def _(i, piece=piece, offset=offset):
                fill(offset + i, jnp.where(odd, piece[i], pieces[0][offset + i]))

            offset += piece.shape[0]

    def transform(quad, spec):
        rows = [
            jnp.concatenate([records[h, pl.ds(quad * 4 + k, segs, stride=spread), :] for h in range(2)], axis=1)
            for k in range(4)
        ]
        spec[...] = lax.dot_general(
            table_ref[...],
            jnp.concatenate(rows, axis=0).astype(jnp.bfloat16),
            (((1,), (1,)), ((), ())),
            preferred_element_type=jnp.float32,
        )

    in_first = lax.broadcasted_iota(jnp.int32, (8, 128), 1) < LEFT

    def whiten(quad, spec):
        for h in range(2):
            a = quad * 4 + 2 * h

            def put(f, real_part, imag_part):
                real_other = pltpu.roll(real_part, LEFT, 1)
                imag_other = pltpu.roll(imag_part, LEFT, 1)
                rows = [
                    (a, jnp.where(in_first, real_part, imag_other)),
                    (OWN + a, jnp.where(in_first, imag_part, -real_other)),
                    (a + 1, jnp.where(in_first, real_other, imag_part)),
                    (OWN + a + 1, jnp.where(in_first, imag_other, -real_part)),
                ]
                for row, value in rows:
                    bins_ref[pl.ds(f * pitch + row, 8, stride=pitch), :] = value

            whiten_tile(spec, slice(h * 128, (h + 1) * 128), put)

    in_turns(OWN // 4, transform, whiten, spec_a, spec_b)

    def copy(group):
        some = pl.ds(group * GROUP, GROUP)
        return pltpu.make_async_copy(packed.at[some], out_ref.at[some], sems.at[group])

    @pl.loop(0, BINS // GROUP)
    def _(group):
        for step in range(GROUP):
            f = group * GROUP + step
            packed[f] = bins_ref[pl.ds(f * pitch, 2 * OWN), :].astype(jnp.bfloat16)
        copy(group).start()

    @pl.loop(0, BINS // GROUP)
    def _(group):
        copy(group).wait()


def left_bins(odd, table, pieces):
    vmem = pl.BlockSpec(memory_space=pltpu.VMEM)
    smem = pl.BlockSpec(memory_space=pltpu.SMEM)
    shape = (BINS, 2 * OWN, 128)
    return pl.pallas_call(
        left_kernel,
        out_shape=jax.ShapeDtypeStruct(shape, jnp.bfloat16),
        in_specs=[smem, vmem] + [pl.BlockSpec(memory_space=pl.ANY)] * len(pieces),
        out_specs=pl.BlockSpec(memory_space=pl.ANY),
        scratch_shapes=[
            pltpu.VMEM((2, pieces[0].shape[0] * (OWN + 1), 128), jnp.float32),
            pltpu.VMEM((512, 256), jnp.float32),
            pltpu.VMEM((512, 256), jnp.float32),
            pltpu.VMEM((BINS * (2 * OWN + 1), 128), jnp.float32),
            pltpu.VMEM(shape, jnp.bfloat16),
            pltpu.SemaphoreType.DMA((BINS // GROUP,)),
            pltpu.SemaphoreType.DMA((len(pieces),)),
        ]
        + [pltpu.VMEM(p.shape, p.dtype) for p in pieces],
        compiler_params=pltpu.CompilerParams(vmem_limit_bytes=48 * MIB),
        cost_estimate=pl.CostEstimate(flops=4_000_000_000, bytes_accessed=8_000_000, transcendentals=0),
        name="left",
    )(odd, table, *pieces)


def lag_sums(table_ref, cross_ref, lags):
    @pl.loop(0, BLK // 8)
    def _(eight):
        for pair in range(4):
            a = 8 * eight + 2 * pair
            for part in range(2):
                cross = jnp.concatenate(
                    [
                        cross_ref[pl.ds((a + k) * PITCH + part * BINS, BINS), :].astype(jnp.bfloat16)
                        for k in range(2)
                    ],
                    axis=1,
                )
                both = jnp.dot(table_ref[part], cross, preferred_element_type=jnp.float32)
                both = both[:HALF] + both[HALF:]
                lags[a, part * HALF:(part + 1) * HALF, :] = both[:, :128]
                lags[a + 1, part * HALF:(part + 1) * HALF, :] = both[:, 128:]


def by_slot(lags, put):
    block = lax.broadcasted_iota(jnp.int32, (BLK, 128), 1) // BLK
    odd_block = {d: (block // d) % 2 == 1 for d in (4, 2, 1)}

    @pl.loop(0, ROWS // (2 * BLK))
    def _(tile):
        for sub in range(2):
            rows = pl.ds(pl.multiple_of((2 * tile + sub) * BLK, BLK), BLK)
            for ha in range(2):
                arrays = [lags[8 * ha + k, rows, :] for k in range(8)]
                for d in (4, 2, 1):
                    for k in range(8):
                        if k & d == 0:
                            one, two = arrays[k], arrays[k + d]
                            arrays[k] = jnp.where(odd_block[d], pltpu.roll(two, BLK * d, 1), one)
                            arrays[k + d] = jnp.where(odd_block[d], two, pltpu.roll(one, 128 - BLK * d, 1))
                for k in range(8):
                    put(k, rows, slice(ha * 128, (ha + 1) * 128), arrays[k])


def gram_kernel(tile, live_ref, first_ref, table_ref, *refs):
    count = 2 + len(CHUNKS)
    sources, outs = refs[:count], refs[count:-count - 3]
    sums, lags, sems = refs[-count - 3:-count]
    own_ref, next_ref, *parts = refs[-count:]
    first = first_ref[...]
    chosen = [jnp.broadcast_to(first == i, (BLK, 128)) for i in range(3)]

    def fetches(block):
        some = pl.ds(block * BLOCK, BLOCK)
        return [
            pltpu.make_async_copy(
                source.at[some] if k < 2 else source.at[tile, some], refs[k - count].at[some], sems.at[k, block]
            )
            for k, source in enumerate(sources)
        ]

    @pl.loop(0, BINS // BLOCK)
    def _(block):
        for fetch in fetches(block):
            fetch.start()

    @pl.loop(0, BINS // BLOCK)
    def _(block):
        for fetch in fetches(block):
            fetch.wait()
        for step in range(BLOCK):
            f = block * BLOCK + step
            right = jnp.concatenate(
                [p[f, part * n:(part + 1) * n, :] for part in range(2) for p, n in zip(parts, CHUNKS)],
                axis=0,
            )
            left = jnp.concatenate([own_ref[f], next_ref[f]], axis=0)
            cross = jnp.dot(left, right, preferred_element_type=jnp.float32)
            for part in range(2):
                starts = [i // 2 * LEFT + part * OWN + i % 2 * BLK for i in range(4)]
                blocks = [cross[start:start + BLK] for start in starts]
                own = blocks[3]
                for i in range(3):
                    own = jnp.where(chosen[i], blocks[i], own)
                for a in range(0, BLK, 8):
                    sums[pl.ds(a * PITCH + part * BINS + f, 8, stride=PITCH), :] = own[a:a + 8]

    lag_sums(table_ref, sums, lags)
    live = [live_ref[8 * tile + q] == 1 for q in range(8)]

    def put(q, rows, lanes, value):
        value = jnp.where(live[q], value, 0.0)
        for out in outs:
            if q < out.shape[0]:
                out[q, rows, lanes] = value.astype(out.dtype)
                return
            q -= out.shape[0]

    by_slot(lags, put)


def gram(tile, live, first, table, left, parts, counts, dtype):
    vmem = pl.BlockSpec(memory_space=pltpu.VMEM)
    arrays = [*left, *parts]
    return pl.pallas_call(
        functools.partial(gram_kernel, tile),
        out_shape=[jax.ShapeDtypeStruct((n, ROWS, 256), dtype) for n in counts],
        in_specs=[pl.BlockSpec(memory_space=pltpu.SMEM), vmem, vmem]
        + [pl.BlockSpec(memory_space=pl.ANY)] * len(arrays),
        out_specs=[vmem] * len(counts),
        scratch_shapes=[
            pltpu.VMEM((BLK * PITCH, 128), jnp.float32),
            pltpu.VMEM((BLK, ROWS, 128), jnp.float32),
            pltpu.SemaphoreType.DMA((len(arrays), BINS // BLOCK)),
        ]
        + [pltpu.VMEM(p.shape[-3:], p.dtype) for p in arrays],
        compiler_params=pltpu.CompilerParams(vmem_limit_bytes=48 * MIB),
        cost_estimate=pl.CostEstimate(flops=16_000_000_000, bytes_accessed=20_000_000, transcendentals=0),
        name="gram",
    )(live, first[:, tile * 128:(tile + 1) * 128], table, *arrays)


def final_kernel(near_any, low_any, high_any, out, near, low, high, later, earlier, sems):
    middle = LAGS // 2
    copies = [
        pltpu.make_async_copy(source, target, sems.at[k])
        for k, (source, target) in enumerate(((near_any, near), (low_any, low), (high_any, high)))
    ]
    for copy in copies:
        copy.start()
    for copy in copies:
        copy.wait()

    @pl.loop(0, HALF // BLK)
    def _(tile):
        start = pl.multiple_of(tile * BLK, BLK)
        for q in range(4):
            far = (low, high)[q // 2]
            even, odd = (
                near[q, rows, :] + far[q % 2, rows, :].astype(jnp.float32)
                for rows in (pl.ds(start, BLK), pl.ds(HALF + start, BLK))
            )
            for h in range(2):
                lanes = slice(h * 128, (h + 1) * 128)
                rows = pl.ds(q * (HALF + 1) + start, BLK)
                later[h, rows, :] = even[:, lanes] + odd[:, lanes]
                earlier[h, rows, :] = even[:, lanes] - odd[:, lanes]

    def put(u):
        slots = pl.ds(u, 4, stride=HALF + 1)
        for h in range(2):
            lanes = slice(h * 128, (h + 1) * 128)
            out[middle + u, :, lanes] = later[h, slots, :]
            out[middle - u, :, lanes] = earlier[h, slots, :]

    @pl.loop(0, middle // 20)
    def _(group):
        for k in range(20):
            put(group * 20 + k)

    put(middle)


def final(near, low, high):
    vmem = pl.BlockSpec(memory_space=pltpu.VMEM)
    return pl.pallas_call(
        final_kernel,
        out_shape=jax.ShapeDtypeStruct((LAGS, 4, 256), jnp.float32),
        in_specs=[pl.BlockSpec(memory_space=pl.ANY)] * 3,
        out_specs=vmem,
        scratch_shapes=[pltpu.VMEM(x.shape, x.dtype) for x in (near, low, high)]
        + [pltpu.VMEM((2, 4 * (HALF + 1), 128), jnp.float32)] * 2
        + [pltpu.SemaphoreType.DMA((3,))],
        compiler_params=pltpu.CompilerParams(vmem_limit_bytes=16 * MIB),
        cost_estimate=pl.CostEstimate(flops=10_000_000, bytes_accessed=7_000_000, transcendentals=0),
        name="final",
    )(near, low, high)


def moved(block, axis, to):
    size = lax.axis_size(axis)
    return lax.ppermute(block, axis, [(i, to(i) % size) for i in range(size)])


def one_chip(block):
    return moved(block, "chan", lambda i: i - 2)


def swap(block):
    return moved(block, "chan", lambda i: i ^ 1)


def first_half(block):
    return moved(block[:, :BLK], "chan", lambda i: i - 1)


def one_row(block, step):
    return moved(block, "tm", lambda i: i + step)


def local(records, pair_blocks, pair_counts):
    segs = records.shape[0]
    table, backward = make_tables(segs * lax.axis_size("tm"))
    owner = lax.axis_index("chan")
    row = lax.axis_index("tm")

    group = np.array([2, 2, 1, 1, 2, 2, 3, 3, 1, 1, 3, 3, 0, 0, 0, 0], np.int32)
    inside = np.array([0, 1, 2, 3, 2, 3, 0, 1, 0, 1, 2, 3, 0, 1, 2, 3], np.int32)
    order = (row + group) % 4 * 4 + inside
    relative = pair_blocks[order] - 2 * owner
    first = jnp.clip(relative[:, 0], 0, 3)
    right = jnp.clip(relative[:, 1], 0, 10)
    live = (order < pair_counts[0]).astype(jnp.int32)
    odd = (owner % 2).astype(jnp.int32)[None]
    first_lanes = jnp.repeat(first, BLK)[None, :]

    barrier = lax.optimization_barrier
    step = CHUNKS[0]
    x_0, later = barrier((records[:step], records))
    x_1 = later[step:]

    def whitened(c, *pieces):
        return whiten_bins(right, odd, table, [records, b0], pieces, c)

    a1_0, a1_1, b0 = one_chip(x_0), one_chip(x_1), swap(records)
    left_own = left_bins(odd, table, [records])
    a1_0, left_own = barrier((a1_0, left_own))
    a2_0, b1_0 = one_chip(a1_0), swap(a1_0)
    a2_1, b1_1 = one_chip(a1_1), swap(a1_1)
    b2_0, o5_0 = swap(a2_0), first_half(a2_0)
    part_0 = whitened(0, a1_0, b1_0, a2_0, b2_0, o5_0)
    a2_1, b1_1, part_0 = barrier((a2_1, b1_1, part_0))
    b2_1, o5_1 = swap(a2_1), first_half(a2_1)
    left_next = left_bins(odd, table, [b0, b1_0, b1_1])
    part_1 = whitened(1, a1_1, b1_1, a2_1, b2_1, o5_1)

    left = [left_own, left_next]
    parts = [part_0, part_1]
    up_out, down_out = gram(0, live, first_lanes, backward, left, parts, (4, 4), jnp.bfloat16)
    from_below, from_above = one_row(up_out, 1), one_row(down_out, -1)
    keep, other, own = gram(1, live, first_lanes, backward, left, parts, (2, 2, 4), jnp.float32)

    f32 = jnp.float32
    two_below = one_row((keep + from_below[:2].astype(f32)).astype(jnp.bfloat16), 1)
    two_above = one_row((other + from_above[:2].astype(f32)).astype(jnp.bfloat16), -1)
    near = own + jnp.concatenate([from_above[2:], from_below[2:]], axis=0).astype(f32)
    return jnp.transpose(final(near, two_below, two_above), (1, 0, 2))


def solution(mesh):
    return jax.shard_map(
        local,
        mesh=mesh,
        in_specs=(P("tm", "chan", None), P("chan", None), P("chan")),
        out_specs=P(("chan", "tm"), None, None),
        check_vma=False,
    )
```

```python
import functools
import math

import jax
import jax.numpy as jnp
import ml_dtypes
import numpy as np
from jax import lax
from jax.experimental import pallas as pl
from jax.experimental.pallas import tpu as pltpu
from jax.sharding import PartitionSpec as P

LAGS = 401
HALF = 208
ROWS = 2 * HALF
BLK = 16
SLOTS = 16
BINS = 256
LEFT = 64
OWN = 32
BAND = 176
CHUNKS = (32, 32)
PITCH = 513
GROUP = 16
BLOCK = 32

water_share = 0.1
tiny_eps = 1e-06

MIB = 1024 * 1024


def make_tables(segments):
    length = 2 * BINS
    index = np.arange(BINS, dtype=np.int32)
    scale = np.float32(2.0 * math.pi / length)
    radians = (index[:, None] * index[None, :] % length).astype(np.float32) * scale
    forward = np.concatenate([np.cos(radians), -np.sin(radians)], axis=1)
    shift = np.arange(HALF, dtype=np.int32)[:, None]
    lag_radians = (shift * index[None, :] % length).astype(np.float32) * scale
    weight = np.where(index == 0, 1.0, 2.0).astype(np.float32)[None, :] / np.float32(
        math.sqrt(float(BINS * segments))
    )
    waves = np.stack([np.cos(lag_radians) * weight, -np.sin(lag_radians) * weight]).astype(np.float32)
    waves[:, LAGS // 2 + 1:] = 0.0
    high = waves.astype(ml_dtypes.bfloat16)
    low = (waves - high.astype(np.float32)).astype(ml_dtypes.bfloat16)
    return (np.ascontiguousarray(forward.astype(ml_dtypes.bfloat16).T), np.concatenate([high, low], axis=1))


def whiten_tiles(spec, put):
    def parts(h, f):
        lanes = slice(h * 128, (h + 1) * 128)
        return spec[f:f + 8, lanes], spec[BINS + f:BINS + f + 8, lanes]

    floors = []
    for h in range(2):
        totals = [None] * 4
        for k, f in enumerate(range(0, BINS, 8)):
            real_part, imag_part = parts(h, f)
            energy = real_part * real_part + imag_part * imag_part
            totals[k % 4] = energy if k < 4 else totals[k % 4] + energy
        total = (totals[0] + totals[1]) + (totals[2] + totals[3])
        level = jnp.sum(total, axis=0, keepdims=True) * (1.0 / BINS)
        floors.append(jnp.broadcast_to(water_share * level + tiny_eps, (8, 128)))
    for f in range(0, BINS, 8):
        for h in range(2):
            real_part, imag_part = parts(h, f)
            inverse = lax.rsqrt(real_part * real_part + imag_part * imag_part + floors[h])
            put(h, f, real_part * inverse, imag_part * inverse)


def in_turns(count, transform, whiten, spec_a, spec_b):
    transform(0, spec_a)

    @pl.loop(0, count // 2)
    def _(pair):
        i = 2 * pair
        transform(i + 1, spec_b)
        whiten(i, spec_a)
        transform(jnp.minimum(i + 2, count - 1), spec_a)
        whiten(i + 1, spec_b)


def whiten_kernel(chunk, right_ref, odd_ref, table_ref, x0, b0, a1, b1, a2, b2, o5, out_ref,
                  band, spec_a, spec_b, bins_ref, packed, sems, band_sems):
    segs = a1.shape[0]
    depth = 2 * segs
    pitch = depth + 1
    odd = odd_ref[0] == 1
    share = pl.ds(chunk * segs, segs)

    def fetch(source, place, channels=32):
        return pltpu.make_async_copy(source, band.at[:, pl.ds(32 * place, channels)], band_sems.at[place])

    fetch(x0.at[share], 0).start()
    fetch(a1, 2).start()
    fetch(a2, 4).start()

    @pl.when(odd)
    def _():
        fetch(b1, 1).start()
        fetch(b2, 3).start()
        fetch(o5, 5, BLK).start()

    @pl.when(jnp.logical_not(odd))
    def _():
        fetch(b0.at[share], 1).start()
        fetch(b1, 3).start()
        fetch(b2.at[:, pl.ds(0, BLK)], 5, BLK).start()

    for place in range(5):
        fetch(a1, place).wait()
    fetch(o5, 5, BLK).wait()

    starts = [pl.multiple_of(right_ref[q] * BLK, BLK) for q in range(SLOTS)]

    def transform(s, spec):
        rows = [band[s, pl.ds(start, BLK), :] for start in starts]
        spec[...] = lax.dot_general(
            table_ref[...],
            jnp.concatenate(rows, axis=0),
            (((1,), (1,)), ((), ())),
            preferred_element_type=jnp.float32,
        )

    def whiten(s, spec):
        def put(h, f, real_part, imag_part):
            bins_ref[h, pl.ds(f * pitch + s, 8, stride=pitch), :] = real_part
            bins_ref[h, pl.ds(f * pitch + segs + s, 8, stride=pitch), :] = imag_part

        whiten_tiles(spec, put)

    in_turns(segs, transform, whiten, spec_a, spec_b)

    def copy(group):
        some = pl.ds(group * GROUP, GROUP)
        return pltpu.make_async_copy(packed.at[:, some], out_ref.at[:, some], sems.at[group])

    @pl.loop(0, BINS // GROUP)
    def _(group):
        for step in range(GROUP):
            f = group * GROUP + step
            for h in range(2):
                packed[h, f] = bins_ref[h, pl.ds(f * pitch, depth), :].astype(jnp.bfloat16)
        copy(group).start()

    @pl.loop(0, BINS // GROUP)
    def _(group):
        copy(group).wait()


def whole(shape):
    return pl.BlockSpec(shape, lambda *_: (0,) * len(shape))


def whiten_bins(right, odd, table, whole_pieces, pieces, chunk):
    smem = pl.BlockSpec(memory_space=pltpu.SMEM)
    anywhere = pl.BlockSpec(memory_space=pl.ANY)
    segs = pieces[0].shape[0]
    shape = (2, BINS, 2 * segs, 128)
    return pl.pallas_call(
        functools.partial(whiten_kernel, chunk),
        out_shape=jax.ShapeDtypeStruct(shape, jnp.bfloat16),
        in_specs=[smem, smem, pl.BlockSpec(memory_space=pltpu.VMEM)] + [anywhere] * (2 + len(pieces)),
        out_specs=pl.BlockSpec(memory_space=pl.ANY),
        scratch_shapes=[
            pltpu.VMEM((segs, BAND, BINS), jnp.bfloat16),
            pltpu.VMEM((512, 256), jnp.float32),
            pltpu.VMEM((512, 256), jnp.float32),
            pltpu.VMEM((2, BINS * (2 * segs + 1), 128), jnp.float32),
            pltpu.VMEM(shape, jnp.bfloat16),
            pltpu.SemaphoreType.DMA((BINS // GROUP,)),
            pltpu.SemaphoreType.DMA((6,)),
        ],
        compiler_params=pltpu.CompilerParams(vmem_limit_bytes=52 * MIB),
        cost_estimate=pl.CostEstimate(flops=240_000_000 * segs, bytes_accessed=8_000_000, transcendentals=0),
        name="whiten",
    )(right, odd, table, *whole_pieces, *pieces)


def left_kernel(odd_ref, table_ref, *refs):
    count = (len(refs) - 8) // 2
    sources, pieces = refs[:count], refs[-count:]
    out_ref, records, spec_a, spec_b, bins_ref, packed, sems, piece_sems = refs[count:-count]
    fetches = [
        pltpu.make_async_copy(source, piece, piece_sems.at[k])
        for k, (source, piece) in enumerate(zip(sources, pieces))
    ]
    for fetch in fetches:
        fetch.start()
    for fetch in fetches:
        fetch.wait()
    odd = odd_ref[0] == 1
    segs = pieces[0].shape[0]
    spread = OWN + 1
    pitch = 2 * OWN + 1

    def fill(s, channels):
        channels = channels.astype(jnp.float32)
        for h in range(2):
            records[h, pl.ds(s * spread, OWN), :] = channels[:, h * 128:(h + 1) * 128]

    if len(pieces) == 1:
        @pl.loop(0, segs)
        def _(s):
            fill(s, pieces[0][s])
    else:
        offset = 0
        for piece in pieces[1:]:
            @pl.loop(0, piece.shape[0])
            def _(i, piece=piece, offset=offset):
                fill(offset + i, jnp.where(odd, piece[i], pieces[0][offset + i]))

            offset += piece.shape[0]

    def transform(quad, spec):
        rows = [
            jnp.concatenate([records[h, pl.ds(quad * 4 + k, segs, stride=spread), :] for h in range(2)], axis=1)
            for k in range(4)
        ]
        spec[...] = lax.dot_general(
            table_ref[...],
            jnp.concatenate(rows, axis=0).astype(jnp.bfloat16),
            (((1,), (1,)), ((), ())),
            preferred_element_type=jnp.float32,
        )

    in_first = lax.broadcasted_iota(jnp.int32, (8, 128), 1) < LEFT

    def whiten(quad, spec):
        def put(h, f, real_part, imag_part):
            a = quad * 4 + 2 * h
            real_other = pltpu.roll(real_part, LEFT, 1)
            imag_other = pltpu.roll(imag_part, LEFT, 1)
            rows = [
                (a, jnp.where(in_first, real_part, imag_other)),
                (OWN + a, jnp.where(in_first, imag_part, -real_other)),
                (a + 1, jnp.where(in_first, real_other, imag_part)),
                (OWN + a + 1, jnp.where(in_first, imag_other, -real_part)),
            ]
            for row, value in rows:
                bins_ref[pl.ds(f * pitch + row, 8, stride=pitch), :] = value

        whiten_tiles(spec, put)

    in_turns(OWN // 4, transform, whiten, spec_a, spec_b)

    def copy(group):
        some = pl.ds(group * GROUP, GROUP)
        return pltpu.make_async_copy(packed.at[some], out_ref.at[some], sems.at[group])

    @pl.loop(0, BINS // GROUP)
    def _(group):
        for step in range(GROUP):
            f = group * GROUP + step
            packed[f] = bins_ref[pl.ds(f * pitch, 2 * OWN), :].astype(jnp.bfloat16)
        copy(group).start()

    @pl.loop(0, BINS // GROUP)
    def _(group):
        copy(group).wait()


def left_bins(odd, table, pieces):
    vmem = pl.BlockSpec(memory_space=pltpu.VMEM)
    smem = pl.BlockSpec(memory_space=pltpu.SMEM)
    shape = (BINS, 2 * OWN, 128)
    return pl.pallas_call(
        left_kernel,
        out_shape=jax.ShapeDtypeStruct(shape, jnp.bfloat16),
        in_specs=[smem, vmem] + [pl.BlockSpec(memory_space=pl.ANY)] * len(pieces),
        out_specs=pl.BlockSpec(memory_space=pl.ANY),
        scratch_shapes=[
            pltpu.VMEM((2, pieces[0].shape[0] * (OWN + 1), 128), jnp.float32),
            pltpu.VMEM((512, 256), jnp.float32),
            pltpu.VMEM((512, 256), jnp.float32),
            pltpu.VMEM((BINS * (2 * OWN + 1), 128), jnp.float32),
            pltpu.VMEM(shape, jnp.bfloat16),
            pltpu.SemaphoreType.DMA((BINS // GROUP,)),
            pltpu.SemaphoreType.DMA((len(pieces),)),
        ]
        + [pltpu.VMEM(p.shape, p.dtype) for p in pieces],
        compiler_params=pltpu.CompilerParams(vmem_limit_bytes=48 * MIB),
        cost_estimate=pl.CostEstimate(flops=4_000_000_000, bytes_accessed=8_000_000, transcendentals=0),
        name="left",
    )(odd, table, *pieces)


def lag_sums(table_ref, cross_ref, lags):
    @pl.loop(0, BLK // 8)
    def _(eight):
        for pair in range(4):
            a = 8 * eight + 2 * pair
            for part in range(2):
                cross = jnp.concatenate(
                    [
                        cross_ref[pl.ds((a + k) * PITCH + part * BINS, BINS), :].astype(jnp.bfloat16)
                        for k in range(2)
                    ],
                    axis=1,
                )
                both = jnp.dot(table_ref[part], cross, preferred_element_type=jnp.float32)
                both = both[:HALF] + both[HALF:]
                lags[a, part * HALF:(part + 1) * HALF, :] = both[:, :128]
                lags[a + 1, part * HALF:(part + 1) * HALF, :] = both[:, 128:]


def by_slot(lags, put):
    block = lax.broadcasted_iota(jnp.int32, (BLK, 128), 1) // BLK
    odd_block = {d: (block // d) % 2 == 1 for d in (4, 2, 1)}

    @pl.loop(0, ROWS // (2 * BLK))
    def _(tile):
        for sub in range(2):
            rows = pl.ds(pl.multiple_of((2 * tile + sub) * BLK, BLK), BLK)
            for ha in range(2):
                arrays = [lags[8 * ha + k, rows, :] for k in range(8)]
                for d in (4, 2, 1):
                    for k in range(8):
                        if k & d == 0:
                            one, two = arrays[k], arrays[k + d]
                            arrays[k] = jnp.where(odd_block[d], pltpu.roll(two, BLK * d, 1), one)
                            arrays[k + d] = jnp.where(odd_block[d], two, pltpu.roll(one, 128 - BLK * d, 1))
                for k in range(8):
                    put(k, rows, slice(ha * 128, (ha + 1) * 128), arrays[k])


def gram_kernel(tile, live_ref, first_ref, table_ref, *refs):
    count = 2 + len(CHUNKS)
    sources, outs = refs[:count], refs[count:-count - 3]
    sums, lags, sems = refs[-count - 3:-count]
    own_ref, next_ref, *parts = refs[-count:]
    first = first_ref[...]
    chosen = [jnp.broadcast_to(first == i, (BLK, 128)) for i in range(3)]

    def fetches(block):
        some = pl.ds(block * BLOCK, BLOCK)
        return [
            pltpu.make_async_copy(
                source.at[some] if k < 2 else source.at[tile, some], refs[k - count].at[some], sems.at[k, block]
            )
            for k, source in enumerate(sources)
        ]

    @pl.loop(0, BINS // BLOCK)
    def _(block):
        for fetch in fetches(block):
            fetch.start()

    @pl.loop(0, BINS // BLOCK)
    def _(block):
        for fetch in fetches(block):
            fetch.wait()
        for step in range(BLOCK):
            f = block * BLOCK + step
            right = jnp.concatenate(
                [p[f, part * n:(part + 1) * n, :] for part in range(2) for p, n in zip(parts, CHUNKS)],
                axis=0,
            )
            left = jnp.concatenate([own_ref[f], next_ref[f]], axis=0)
            cross = jnp.dot(left, right, preferred_element_type=jnp.float32)
            for part in range(2):
                starts = [i // 2 * LEFT + part * OWN + i % 2 * BLK for i in range(4)]
                blocks = [cross[start:start + BLK] for start in starts]
                own = blocks[3]
                for i in range(3):
                    own = jnp.where(chosen[i], blocks[i], own)
                for a in range(0, BLK, 8):
                    sums[pl.ds(a * PITCH + part * BINS + f, 8, stride=PITCH), :] = own[a:a + 8]

    lag_sums(table_ref, sums, lags)
    live = [live_ref[8 * tile + q] == 1 for q in range(8)]

    def put(q, rows, lanes, value):
        value = jnp.where(live[q], value, 0.0)
        for out in outs:
            if q < out.shape[0]:
                out[q, rows, lanes] = value.astype(out.dtype)
                return
            q -= out.shape[0]

    by_slot(lags, put)


def gram(tile, live, first, table, left, parts, counts, dtype):
    vmem = pl.BlockSpec(memory_space=pltpu.VMEM)
    arrays = [*left, *parts]
    return pl.pallas_call(
        functools.partial(gram_kernel, tile),
        out_shape=[jax.ShapeDtypeStruct((n, ROWS, 256), dtype) for n in counts],
        in_specs=[pl.BlockSpec(memory_space=pltpu.SMEM), vmem, vmem]
        + [pl.BlockSpec(memory_space=pl.ANY)] * len(arrays),
        out_specs=[vmem] * len(counts),
        scratch_shapes=[
            pltpu.VMEM((BLK * PITCH, 128), jnp.float32),
            pltpu.VMEM((BLK, ROWS, 128), jnp.float32),
            pltpu.SemaphoreType.DMA((len(arrays), BINS // BLOCK)),
        ]
        + [pltpu.VMEM(p.shape[-3:], p.dtype) for p in arrays],
        compiler_params=pltpu.CompilerParams(vmem_limit_bytes=48 * MIB),
        cost_estimate=pl.CostEstimate(flops=16_000_000_000, bytes_accessed=20_000_000, transcendentals=0),
        name="gram",
    )(live, first[:, tile * 128:(tile + 1) * 128], table, *arrays)


def final_kernel(near_any, low_any, high_any, out, near, low, high, later, earlier, sems):
    middle = LAGS // 2
    copies = [
        pltpu.make_async_copy(source, target, sems.at[k])
        for k, (source, target) in enumerate(((near_any, near), (low_any, low), (high_any, high)))
    ]
    for copy in copies:
        copy.start()
    for copy in copies:
        copy.wait()

    @pl.loop(0, HALF // BLK)
    def _(tile):
        start = pl.multiple_of(tile * BLK, BLK)
        for q in range(4):
            far = (low, high)[q // 2]
            even, odd = (
                near[q, rows, :] + far[q % 2, rows, :].astype(jnp.float32)
                for rows in (pl.ds(start, BLK), pl.ds(HALF + start, BLK))
            )
            for h in range(2):
                lanes = slice(h * 128, (h + 1) * 128)
                rows = pl.ds(q * (HALF + 1) + start, BLK)
                later[h, rows, :] = even[:, lanes] + odd[:, lanes]
                earlier[h, rows, :] = even[:, lanes] - odd[:, lanes]

    def put(u):
        slots = pl.ds(u, 4, stride=HALF + 1)
        for h in range(2):
            lanes = slice(h * 128, (h + 1) * 128)
            out[middle + u, :, lanes] = later[h, slots, :]
            out[middle - u, :, lanes] = earlier[h, slots, :]

    @pl.loop(0, middle // 20)
    def _(group):
        for k in range(20):
            put(group * 20 + k)

    put(middle)


def final(near, low, high):
    vmem = pl.BlockSpec(memory_space=pltpu.VMEM)
    return pl.pallas_call(
        final_kernel,
        out_shape=jax.ShapeDtypeStruct((LAGS, 4, 256), jnp.float32),
        in_specs=[pl.BlockSpec(memory_space=pl.ANY)] * 3,
        out_specs=vmem,
        scratch_shapes=[pltpu.VMEM(x.shape, x.dtype) for x in (near, low, high)]
        + [pltpu.VMEM((2, 4 * (HALF + 1), 128), jnp.float32)] * 2
        + [pltpu.SemaphoreType.DMA((3,))],
        compiler_params=pltpu.CompilerParams(vmem_limit_bytes=16 * MIB),
        cost_estimate=pl.CostEstimate(flops=10_000_000, bytes_accessed=7_000_000, transcendentals=0),
        name="final",
    )(near, low, high)


def moved(block, axis, to):
    size = lax.axis_size(axis)
    return lax.ppermute(block, axis, [(i, to(i) % size) for i in range(size)])


def one_chip(block):
    return moved(block, "chan", lambda i: i - 2)


def swap(block):
    return moved(block, "chan", lambda i: i ^ 1)


def first_half(block):
    return moved(block[:, :BLK], "chan", lambda i: i - 1)


def one_row(block, step):
    return moved(block, "tm", lambda i: i + step)


def local(records, pair_blocks, pair_counts):
    segs = records.shape[0]
    table, backward = make_tables(segs * lax.axis_size("tm"))
    owner = lax.axis_index("chan")
    row = lax.axis_index("tm")

    group = np.array([2, 2, 1, 1, 2, 2, 3, 3, 1, 1, 3, 3, 0, 0, 0, 0], np.int32)
    inside = np.array([0, 1, 2, 3, 2, 3, 0, 1, 0, 1, 2, 3, 0, 1, 2, 3], np.int32)
    order = (row + group) % 4 * 4 + inside
    relative = pair_blocks[order] - 2 * owner
    first = jnp.clip(relative[:, 0], 0, 3)
    right = jnp.clip(relative[:, 1], 0, 10)
    live = (order < pair_counts[0]).astype(jnp.int32)
    odd = (owner % 2).astype(jnp.int32)[None]
    first_lanes = jnp.repeat(first, BLK)[None, :]

    barrier = lax.optimization_barrier
    step = CHUNKS[0]
    x_0, later = barrier((records[:step], records))
    x_1 = later[step:]

    def whitened(c, *pieces):
        return whiten_bins(right, odd, table, [records, b0], pieces, c)

    a1_0, a1_1, b0 = one_chip(x_0), one_chip(x_1), swap(records)
    left_own = left_bins(odd, table, [records])
    a1_0, left_own = barrier((a1_0, left_own))
    a2_0, b1_0 = one_chip(a1_0), swap(a1_0)
    a2_1, b1_1 = one_chip(a1_1), swap(a1_1)
    b2_0, o5_0 = swap(a2_0), first_half(a2_0)
    part_0 = whitened(0, a1_0, b1_0, a2_0, b2_0, o5_0)
    a2_1, b1_1, part_0 = barrier((a2_1, b1_1, part_0))
    b2_1, o5_1 = swap(a2_1), first_half(a2_1)
    left_next = left_bins(odd, table, [b0, b1_0, b1_1])
    part_1 = whitened(1, a1_1, b1_1, a2_1, b2_1, o5_1)

    left = [left_own, left_next]
    parts = [part_0, part_1]
    up_out, down_out = gram(0, live, first_lanes, backward, left, parts, (4, 4), jnp.bfloat16)
    from_below, from_above = one_row(up_out, 1), one_row(down_out, -1)
    keep, other, own = gram(1, live, first_lanes, backward, left, parts, (2, 2, 4), jnp.float32)

    f32 = jnp.float32
    two_below = one_row((keep + from_below[:2].astype(f32)).astype(jnp.bfloat16), 1)
    two_above = one_row((other + from_above[:2].astype(f32)).astype(jnp.bfloat16), -1)
    near = own + jnp.concatenate([from_above[2:], from_below[2:]], axis=0).astype(f32)
    return jnp.transpose(final(near, two_below, two_above), (1, 0, 2))


def solution(mesh):
    return jax.shard_map(
        local,
        mesh=mesh,
        in_specs=(P("tm", "chan", None), P("chan", None), P("chan")),
        out_specs=P(("chan", "tm"), None, None),
        check_vma=False,
    )
```

```python
import functools
import math

import jax
import jax.numpy as jnp
import ml_dtypes
import numpy as np
from jax import lax
from jax.experimental import pallas as pl
from jax.experimental.pallas import tpu as pltpu
from jax.sharding import PartitionSpec as P

LAGS = 401
HALF = 208
ROWS = 2 * HALF
BLK = 16
SLOTS = 16
BINS = 256
LEFT = 64
OWN = 32
BAND = 176
CHUNKS = (32, 32)
PITCH = 513
GROUP = 16
BLOCK = 32

water_share = 0.1
tiny_eps = 1e-06

MIB = 1024 * 1024


def make_tables(segments):
    length = 2 * BINS
    index = np.arange(BINS, dtype=np.int32)
    scale = np.float32(2.0 * math.pi / length)
    radians = (index[:, None] * index[None, :] % length).astype(np.float32) * scale
    forward = np.concatenate([np.cos(radians), -np.sin(radians)], axis=1)
    shift = np.arange(HALF, dtype=np.int32)[:, None]
    lag_radians = (shift * index[None, :] % length).astype(np.float32) * scale
    weight = np.where(index == 0, 1.0, 2.0).astype(np.float32)[None, :] / np.float32(
        math.sqrt(float(BINS * segments))
    )
    waves = np.stack([np.cos(lag_radians) * weight, -np.sin(lag_radians) * weight]).astype(np.float32)
    waves[:, LAGS // 2 + 1:] = 0.0
    high = waves.astype(ml_dtypes.bfloat16)
    low = (waves - high.astype(np.float32)).astype(ml_dtypes.bfloat16)
    return (np.ascontiguousarray(forward.astype(ml_dtypes.bfloat16).T), np.concatenate([high, low], axis=1))


def whiten_tile(spec, lanes, put):
    total = jnp.zeros((8, 128), jnp.float32)
    for f in range(0, BINS, 8):
        real_part = spec[f:f + 8, lanes]
        imag_part = spec[BINS + f:BINS + f + 8, lanes]
        total = total + (real_part * real_part + imag_part * imag_part)
    level = jnp.sum(total, axis=0, keepdims=True) * (1.0 / BINS)
    floor = jnp.broadcast_to(water_share * level + tiny_eps, (8, 128))
    for f in range(0, BINS, 8):
        real_part = spec[f:f + 8, lanes]
        imag_part = spec[BINS + f:BINS + f + 8, lanes]
        inverse = lax.rsqrt(real_part * real_part + imag_part * imag_part + floor)
        put(f, real_part * inverse, imag_part * inverse)


def in_turns(count, transform, whiten, spec_a, spec_b):
    transform(0, spec_a)

    @pl.loop(0, count // 2)
    def _(pair):
        i = 2 * pair
        transform(i + 1, spec_b)
        whiten(i, spec_a)
        transform(jnp.minimum(i + 2, count - 1), spec_a)
        whiten(i + 1, spec_b)


def whiten_kernel(chunk, right_ref, odd_ref, table_ref, x0, b0, a1, b1, a2, b2, o5, out_ref,
                  band, spec_a, spec_b, bins_ref, packed, sems, band_sems):
    segs = a1.shape[0]
    depth = 2 * segs
    pitch = depth + 1
    odd = odd_ref[0] == 1
    share = pl.ds(chunk * segs, segs)

    def fetch(source, place, channels=32):
        return pltpu.make_async_copy(source, band.at[:, pl.ds(32 * place, channels)], band_sems.at[place])

    fetch(x0.at[share], 0).start()
    fetch(a1, 2).start()
    fetch(a2, 4).start()

    @pl.when(odd)
    def _():
        fetch(b1, 1).start()
        fetch(b2, 3).start()
        fetch(o5, 5, BLK).start()

    @pl.when(jnp.logical_not(odd))
    def _():
        fetch(b0.at[share], 1).start()
        fetch(b1, 3).start()
        fetch(b2.at[:, pl.ds(0, BLK)], 5, BLK).start()

    for place in range(5):
        fetch(a1, place).wait()
    fetch(o5, 5, BLK).wait()

    starts = [pl.multiple_of(right_ref[q] * BLK, BLK) for q in range(SLOTS)]

    def transform(s, spec):
        rows = [band[s, pl.ds(start, BLK), :] for start in starts]
        spec[...] = lax.dot_general(
            table_ref[...],
            jnp.concatenate(rows, axis=0),
            (((1,), (1,)), ((), ())),
            preferred_element_type=jnp.float32,
        )

    def whiten(s, spec):
        for h in range(2):
            def put(f, real_part, imag_part):
                bins_ref[h, pl.ds(f * pitch + s, 8, stride=pitch), :] = real_part
                bins_ref[h, pl.ds(f * pitch + segs + s, 8, stride=pitch), :] = imag_part

            whiten_tile(spec, slice(h * 128, (h + 1) * 128), put)

    in_turns(segs, transform, whiten, spec_a, spec_b)

    def copy(group):
        some = pl.ds(group * GROUP, GROUP)
        return pltpu.make_async_copy(packed.at[:, some], out_ref.at[:, some], sems.at[group])

    @pl.loop(0, BINS // GROUP)
    def _(group):
        for step in range(GROUP):
            f = group * GROUP + step
            for h in range(2):
                packed[h, f] = bins_ref[h, pl.ds(f * pitch, depth), :].astype(jnp.bfloat16)
        copy(group).start()

    @pl.loop(0, BINS // GROUP)
    def _(group):
        copy(group).wait()


def whole(shape):
    return pl.BlockSpec(shape, lambda *_: (0,) * len(shape))


def whiten_bins(right, odd, table, whole_pieces, pieces, chunk):
    smem = pl.BlockSpec(memory_space=pltpu.SMEM)
    anywhere = pl.BlockSpec(memory_space=pl.ANY)
    segs = pieces[0].shape[0]
    shape = (2, BINS, 2 * segs, 128)
    return pl.pallas_call(
        functools.partial(whiten_kernel, chunk),
        out_shape=jax.ShapeDtypeStruct(shape, jnp.bfloat16),
        in_specs=[smem, smem, pl.BlockSpec(memory_space=pltpu.VMEM)] + [anywhere] * (2 + len(pieces)),
        out_specs=pl.BlockSpec(memory_space=pl.ANY),
        scratch_shapes=[
            pltpu.VMEM((segs, BAND, BINS), jnp.bfloat16),
            pltpu.VMEM((512, 256), jnp.float32),
            pltpu.VMEM((512, 256), jnp.float32),
            pltpu.VMEM((2, BINS * (2 * segs + 1), 128), jnp.float32),
            pltpu.VMEM(shape, jnp.bfloat16),
            pltpu.SemaphoreType.DMA((BINS // GROUP,)),
            pltpu.SemaphoreType.DMA((6,)),
        ],
        compiler_params=pltpu.CompilerParams(vmem_limit_bytes=52 * MIB),
        cost_estimate=pl.CostEstimate(flops=240_000_000 * segs, bytes_accessed=8_000_000, transcendentals=0),
        name="whiten",
    )(right, odd, table, *whole_pieces, *pieces)


def left_kernel(odd_ref, table_ref, *refs):
    count = (len(refs) - 8) // 2
    sources, pieces = refs[:count], refs[-count:]
    out_ref, records, spec_a, spec_b, bins_ref, packed, sems, piece_sems = refs[count:-count]
    fetches = [
        pltpu.make_async_copy(source, piece, piece_sems.at[k])
        for k, (source, piece) in enumerate(zip(sources, pieces))
    ]
    for fetch in fetches:
        fetch.start()
    for fetch in fetches:
        fetch.wait()
    odd = odd_ref[0] == 1
    segs = pieces[0].shape[0]
    spread = OWN + 1
    pitch = 2 * OWN + 1

    def fill(s, channels):
        channels = channels.astype(jnp.float32)
        for h in range(2):
            records[h, pl.ds(s * spread, OWN), :] = channels[:, h * 128:(h + 1) * 128]

    if len(pieces) == 1:
        @pl.loop(0, segs)
        def _(s):
            fill(s, pieces[0][s])
    else:
        offset = 0
        for piece in pieces[1:]:
            @pl.loop(0, piece.shape[0])
            def _(i, piece=piece, offset=offset):
                fill(offset + i, jnp.where(odd, piece[i], pieces[0][offset + i]))

            offset += piece.shape[0]

    def transform(quad, spec):
        rows = [
            jnp.concatenate([records[h, pl.ds(quad * 4 + k, segs, stride=spread), :] for h in range(2)], axis=1)
            for k in range(4)
        ]
        spec[...] = lax.dot_general(
            table_ref[...],
            jnp.concatenate(rows, axis=0).astype(jnp.bfloat16),
            (((1,), (1,)), ((), ())),
            preferred_element_type=jnp.float32,
        )

    in_first = lax.broadcasted_iota(jnp.int32, (8, 128), 1) < LEFT

    def whiten(quad, spec):
        for h in range(2):
            a = quad * 4 + 2 * h

            def put(f, real_part, imag_part):
                real_other = pltpu.roll(real_part, LEFT, 1)
                imag_other = pltpu.roll(imag_part, LEFT, 1)
                rows = [
                    (a, jnp.where(in_first, real_part, imag_other)),
                    (OWN + a, jnp.where(in_first, imag_part, -real_other)),
                    (a + 1, jnp.where(in_first, real_other, imag_part)),
                    (OWN + a + 1, jnp.where(in_first, imag_other, -real_part)),
                ]
                for row, value in rows:
                    bins_ref[pl.ds(f * pitch + row, 8, stride=pitch), :] = value

            whiten_tile(spec, slice(h * 128, (h + 1) * 128), put)

    in_turns(OWN // 4, transform, whiten, spec_a, spec_b)

    def copy(group):
        some = pl.ds(group * GROUP, GROUP)
        return pltpu.make_async_copy(packed.at[some], out_ref.at[some], sems.at[group])

    @pl.loop(0, BINS // GROUP)
    def _(group):
        for step in range(GROUP):
            f = group * GROUP + step
            packed[f] = bins_ref[pl.ds(f * pitch, 2 * OWN), :].astype(jnp.bfloat16)
        copy(group).start()

    @pl.loop(0, BINS // GROUP)
    def _(group):
        copy(group).wait()


def left_bins(odd, table, pieces):
    vmem = pl.BlockSpec(memory_space=pltpu.VMEM)
    smem = pl.BlockSpec(memory_space=pltpu.SMEM)
    shape = (BINS, 2 * OWN, 128)
    return pl.pallas_call(
        left_kernel,
        out_shape=jax.ShapeDtypeStruct(shape, jnp.bfloat16),
        in_specs=[smem, vmem] + [pl.BlockSpec(memory_space=pl.ANY)] * len(pieces),
        out_specs=pl.BlockSpec(memory_space=pl.ANY),
        scratch_shapes=[
            pltpu.VMEM((2, pieces[0].shape[0] * (OWN + 1), 128), jnp.float32),
            pltpu.VMEM((512, 256), jnp.float32),
            pltpu.VMEM((512, 256), jnp.float32),
            pltpu.VMEM((BINS * (2 * OWN + 1), 128), jnp.float32),
            pltpu.VMEM(shape, jnp.bfloat16),
            pltpu.SemaphoreType.DMA((BINS // GROUP,)),
            pltpu.SemaphoreType.DMA((len(pieces),)),
        ]
        + [pltpu.VMEM(p.shape, p.dtype) for p in pieces],
        compiler_params=pltpu.CompilerParams(vmem_limit_bytes=58 * MIB),
        cost_estimate=pl.CostEstimate(flops=4_000_000_000, bytes_accessed=8_000_000, transcendentals=0),
        name="left",
    )(odd, table, *pieces)


def lag_sums(table_ref, cross_ref, lags):
    @pl.loop(0, BLK // 8)
    def _(eight):
        for pair in range(4):
            a = 8 * eight + 2 * pair
            for part in range(2):
                cross = jnp.concatenate(
                    [
                        cross_ref[pl.ds((a + k) * PITCH + part * BINS, BINS), :].astype(jnp.bfloat16)
                        for k in range(2)
                    ],
                    axis=1,
                )
                both = jnp.dot(table_ref[part], cross, preferred_element_type=jnp.float32)
                both = both[:HALF] + both[HALF:]
                lags[a, part * HALF:(part + 1) * HALF, :] = both[:, :128]
                lags[a + 1, part * HALF:(part + 1) * HALF, :] = both[:, 128:]


def by_slot(lags, put):
    block = lax.broadcasted_iota(jnp.int32, (BLK, 128), 1) // BLK
    odd_block = {d: (block // d) % 2 == 1 for d in (4, 2, 1)}

    @pl.loop(0, ROWS // (2 * BLK))
    def _(tile):
        for sub in range(2):
            rows = pl.ds(pl.multiple_of((2 * tile + sub) * BLK, BLK), BLK)
            for ha in range(2):
                arrays = [lags[8 * ha + k, rows, :] for k in range(8)]
                for d in (4, 2, 1):
                    for k in range(8):
                        if k & d == 0:
                            one, two = arrays[k], arrays[k + d]
                            arrays[k] = jnp.where(odd_block[d], pltpu.roll(two, BLK * d, 1), one)
                            arrays[k + d] = jnp.where(odd_block[d], two, pltpu.roll(one, 128 - BLK * d, 1))
                for k in range(8):
                    put(k, rows, slice(ha * 128, (ha + 1) * 128), arrays[k])


def gram_kernel(tile, live_ref, first_ref, table_ref, *refs):
    count = 2 + len(CHUNKS)
    sources, outs = refs[:count], refs[count:-count - 3]
    sums, lags, sems = refs[-count - 3:-count]
    own_ref, next_ref, *parts = refs[-count:]
    first = first_ref[...]
    chosen = [jnp.broadcast_to(first == i, (BLK, 128)) for i in range(3)]

    def fetches(block):
        some = pl.ds(block * BLOCK, BLOCK)
        return [
            pltpu.make_async_copy(
                source.at[some] if k < 2 else source.at[tile, some], refs[k - count].at[some], sems.at[k, block]
            )
            for k, source in enumerate(sources)
        ]

    @pl.loop(0, BINS // BLOCK)
    def _(block):
        for fetch in fetches(block):
            fetch.start()

    @pl.loop(0, BINS // BLOCK)
    def _(block):
        for fetch in fetches(block):
            fetch.wait()
        for step in range(BLOCK):
            f = block * BLOCK + step
            right = jnp.concatenate(
                [p[f, part * n:(part + 1) * n, :] for part in range(2) for p, n in zip(parts, CHUNKS)],
                axis=0,
            )
            left = jnp.concatenate([own_ref[f], next_ref[f]], axis=0)
            cross = jnp.dot(left, right, preferred_element_type=jnp.float32)
            for part in range(2):
                starts = [i // 2 * LEFT + part * OWN + i % 2 * BLK for i in range(4)]
                blocks = [cross[start:start + BLK] for start in starts]
                own = blocks[3]
                for i in range(3):
                    own = jnp.where(chosen[i], blocks[i], own)
                for a in range(0, BLK, 8):
                    sums[pl.ds(a * PITCH + part * BINS + f, 8, stride=PITCH), :] = own[a:a + 8]

    lag_sums(table_ref, sums, lags)
    live = [live_ref[8 * tile + q] == 1 for q in range(8)]

    def put(q, rows, lanes, value):
        value = jnp.where(live[q], value, 0.0)
        for out in outs:
            if q < out.shape[0]:
                out[q, rows, lanes] = value.astype(out.dtype)
                return
            q -= out.shape[0]

    by_slot(lags, put)


def gram(tile, live, first, table, left, parts, counts, dtype):
    vmem = pl.BlockSpec(memory_space=pltpu.VMEM)
    arrays = [*left, *parts]
    return pl.pallas_call(
        functools.partial(gram_kernel, tile),
        out_shape=[jax.ShapeDtypeStruct((n, ROWS, 256), dtype) for n in counts],
        in_specs=[pl.BlockSpec(memory_space=pltpu.SMEM), vmem, vmem]
        + [pl.BlockSpec(memory_space=pl.ANY)] * len(arrays),
        out_specs=[vmem] * len(counts),
        scratch_shapes=[
            pltpu.VMEM((BLK * PITCH, 128), jnp.float32),
            pltpu.VMEM((BLK, ROWS, 128), jnp.float32),
            pltpu.SemaphoreType.DMA((len(arrays), BINS // BLOCK)),
        ]
        + [pltpu.VMEM(p.shape[-3:], p.dtype) for p in arrays],
        compiler_params=pltpu.CompilerParams(vmem_limit_bytes=48 * MIB),
        cost_estimate=pl.CostEstimate(flops=16_000_000_000, bytes_accessed=20_000_000, transcendentals=0),
        name="gram",
    )(live, first[:, tile * 128:(tile + 1) * 128], table, *arrays)


def final_kernel(near_any, low_any, high_any, out, near, low, high, later, earlier, sems):
    middle = LAGS // 2
    copies = [
        pltpu.make_async_copy(source, target, sems.at[k])
        for k, (source, target) in enumerate(((near_any, near), (low_any, low), (high_any, high)))
    ]
    for copy in copies:
        copy.start()
    for copy in copies:
        copy.wait()

    @pl.loop(0, HALF // BLK)
    def _(tile):
        start = pl.multiple_of(tile * BLK, BLK)
        for q in range(4):
            far = (low, high)[q // 2]
            even, odd = (
                near[q, rows, :] + far[q % 2, rows, :].astype(jnp.float32)
                for rows in (pl.ds(start, BLK), pl.ds(HALF + start, BLK))
            )
            for h in range(2):
                lanes = slice(h * 128, (h + 1) * 128)
                rows = pl.ds(q * (HALF + 1) + start, BLK)
                later[h, rows, :] = even[:, lanes] + odd[:, lanes]
                earlier[h, rows, :] = even[:, lanes] - odd[:, lanes]

    def put(u):
        slots = pl.ds(u, 4, stride=HALF + 1)
        for h in range(2):
            lanes = slice(h * 128, (h + 1) * 128)
            out[middle + u, :, lanes] = later[h, slots, :]
            out[middle - u, :, lanes] = earlier[h, slots, :]

    @pl.loop(0, middle // 20)
    def _(group):
        for k in range(20):
            put(group * 20 + k)

    put(middle)


def final(near, low, high):
    vmem = pl.BlockSpec(memory_space=pltpu.VMEM)
    return pl.pallas_call(
        final_kernel,
        out_shape=jax.ShapeDtypeStruct((LAGS, 4, 256), jnp.float32),
        in_specs=[pl.BlockSpec(memory_space=pl.ANY)] * 3,
        out_specs=vmem,
        scratch_shapes=[pltpu.VMEM(x.shape, x.dtype) for x in (near, low, high)]
        + [pltpu.VMEM((2, 4 * (HALF + 1), 128), jnp.float32)] * 2
        + [pltpu.SemaphoreType.DMA((3,))],
        compiler_params=pltpu.CompilerParams(vmem_limit_bytes=16 * MIB),
        cost_estimate=pl.CostEstimate(flops=10_000_000, bytes_accessed=7_000_000, transcendentals=0),
        name="final",
    )(near, low, high)


def moved(block, axis, to):
    size = lax.axis_size(axis)
    return lax.ppermute(block, axis, [(i, to(i) % size) for i in range(size)])


def one_chip(block):
    return moved(block, "chan", lambda i: i - 2)


def swap(block):
    return moved(block, "chan", lambda i: i ^ 1)


def first_half(block):
    return moved(block[:, :BLK], "chan", lambda i: i - 1)


def one_row(block, step):
    return moved(block, "tm", lambda i: i + step)


def local(records, pair_blocks, pair_counts):
    segs = records.shape[0]
    table, backward = make_tables(segs * lax.axis_size("tm"))
    owner = lax.axis_index("chan")
    row = lax.axis_index("tm")

    group = np.array([2, 2, 1, 1, 2, 2, 3, 3, 1, 1, 3, 3, 0, 0, 0, 0], np.int32)
    inside = np.array([0, 1, 2, 3, 2, 3, 0, 1, 0, 1, 2, 3, 0, 1, 2, 3], np.int32)
    order = (row + group) % 4 * 4 + inside
    relative = pair_blocks[order] - 2 * owner
    first = jnp.clip(relative[:, 0], 0, 3)
    right = jnp.clip(relative[:, 1], 0, 10)
    live = (order < pair_counts[0]).astype(jnp.int32)
    odd = (owner % 2).astype(jnp.int32)[None]
    first_lanes = jnp.repeat(first, BLK)[None, :]

    barrier = lax.optimization_barrier
    step = CHUNKS[0]
    x_0, later = barrier((records[:step], records))
    x_1 = later[step:]

    def whitened(c, *pieces):
        return whiten_bins(right, odd, table, [records, b0], pieces, c)

    a1_0, a1_1, b0 = one_chip(x_0), one_chip(x_1), swap(records)
    left_own = left_bins(odd, table, [records])
    a1_0, left_own = barrier((a1_0, left_own))
    a2_0, b1_0 = one_chip(a1_0), swap(a1_0)
    a2_1, b1_1 = one_chip(a1_1), swap(a1_1)
    b2_0, o5_0 = swap(a2_0), first_half(a2_0)
    part_0 = whitened(0, a1_0, b1_0, a2_0, b2_0, o5_0)
    a2_1, b1_1, part_0 = barrier((a2_1, b1_1, part_0))
    b2_1, o5_1 = swap(a2_1), first_half(a2_1)
    left_next = left_bins(odd, table, [b0, b1_0, b1_1])
    part_1 = whitened(1, a1_1, b1_1, a2_1, b2_1, o5_1)

    left = [left_own, left_next]
    parts = [part_0, part_1]
    up_out, down_out = gram(0, live, first_lanes, backward, left, parts, (4, 4), jnp.bfloat16)
    from_below, from_above = one_row(up_out, 1), one_row(down_out, -1)
    keep, other, own = gram(1, live, first_lanes, backward, left, parts, (2, 2, 4), jnp.float32)

    f32 = jnp.float32
    two_below = one_row((keep + from_below[:2].astype(f32)).astype(jnp.bfloat16), 1)
    two_above = one_row((other + from_above[:2].astype(f32)).astype(jnp.bfloat16), -1)
    near = own + jnp.concatenate([from_above[2:], from_below[2:]], axis=0).astype(f32)
    return jnp.transpose(final(near, two_below, two_above), (1, 0, 2))


def solution(mesh):
    return jax.shard_map(
        local,
        mesh=mesh,
        in_specs=(P("tm", "chan", None), P("chan", None), P("chan")),
        out_specs=P(("chan", "tm"), None, None),
        check_vma=False,
    )
```
